256 devices in a mesh: cfg: 2 (over y_hi), uly: 8 (over x, core), blk: 16 (over y_lo, z).
Axes of the slice: x: 4, y: 4 (y_hi: 2, y_lo: 2; y = y_hi * 2 + y_lo), z: 8, core: 2. Of those that a mesh axis runs over, the one named last changes fastest.
Arguments:
- hidden: bfloat16 [2, 8192, 3072], P('cfg', ('uly', 'blk')), may hold values from -400 to 400
- final_mod: float32 [2, 2, 3072], P('cfg'), may hold values from -3 to 3
- final_weight: bfloat16 [3072, 64], replicated, may hold values from -0.109375 to 0.109375
- latent: float32 [8192, 64], P(('uly', 'blk')), may hold values from -6 to 6
- guidance: float32 [50], replicated, may hold values from 2 to 6
- step_size: float32 [50], replicated, may hold values from 0.1 to 0.4
- step_index: int32 [1], replicated, may hold values from 0 to 49
- embed_weight: float32 [64, 3072], replicated, may hold values from -0.75 to 0.75
- block_mod: float32 [2, 2, 3072], P('cfg'), may hold values from -3 to 3
- qkv_weight: bfloat16 [3072, 3, 3072], P(None, None, 'uly'), may hold values from -0.109375 to 0.109375
- qk_gains: float32 [2, 128], replicated, may hold values from 0.25 to 1.75
Outputs:
- next_latent: float32 [8192, 64], P(('uly', 'blk'))
- attention: bfloat16 [2, 8192, 3072], P('cfg', ('uly', 'blk'))
The draws below stay inside these ranges and needn't reach their ends.
Inputs may be any that keep to these rules, and one draw needn't show every extreme that they name: `step_index`: index of the current denoising step.
All inputs are finite; a program needn't handle non-finite values.
Results may differ from the reference program's by a relative error of at most 0.007.
Values may be sent and summed in bfloat16 or wider, within the bound.
A program may use at most 128 MiB of HBM per device.

```python
import jax
import jax.numpy as jnp
from jax import lax

HEADS = 24
HEAD_DIM = 128
CHAN = 64
STEPS = 50
GRID_H = 32
GRID_W = 32
D = 3072
TOKENS = 8192


def draw_hidden(key, part):
    key = jax.random.fold_in(key, 7)
    first, second, third = jax.random.split(key, 3)
    row_scale = jnp.exp(jax.random.uniform(first, (2, TOKENS, 1), jnp.float32) * jnp.log(10.0))
    col_scale = jnp.exp(jax.random.uniform(second, (1, 1, D), jnp.float32) * jnp.log(10.0))
    base = jax.random.normal(third, (2, TOKENS, D), jnp.float32)
    values = jnp.clip(base * row_scale * col_scale * 0.25, -400.0, 400.0)
    return values.astype(jnp.bfloat16)


def level_of(stream_key, extent, shards, smallest, top_value):
    level, own = 1.0, jax.random.fold_in(stream_key, 6)
    for axis_at, parts in shards:
        steps = jnp.exp(jax.random.uniform(jax.random.fold_in(own, axis_at), (parts,), jnp.float32, smallest / len(shards), top_value / len(shards)))
        level = level * jnp.repeat(steps, extent[axis_at] // parts).reshape([-1 if axis == axis_at else 1 for axis in range(len(extent))])
    return level


def normal_values(stream_key, extent, spread, most, cuts=(), kind=jnp.bfloat16):
    drawn = jax.random.normal(stream_key, extent, jnp.float32) * spread
    if len(cuts) > 0:
        drawn = level_of(stream_key, extent, cuts, -0.22, 0.18) * drawn
    return jnp.clip(drawn, min=-most, max=most).astype(kind)


def setup_inputs(seed: int = 0) -> dict:
    key_list = jax.random.split(jax.random.key(seed), 12)
    hidden = draw_hidden(jax.random.fold_in(key_list[11], 71), 0)
    final_mod = normal_values(key_list[1], (2, 2, D), 0.5, 3.0, ((0, 2),), jnp.float32)
    final_weight = normal_values(key_list[2], (D, CHAN), D ** -0.5, 0.109375)
    latent = normal_values(key_list[3], (TOKENS, CHAN), 1.0, 6.0, ((0, 128),), jnp.float32)
    guidance = jnp.clip(jax.random.uniform(key_list[4], (STEPS,), jnp.float32, 2.0, 6.0), 2.0, 6.0)
    step_size = jnp.clip(jax.random.uniform(key_list[5], (STEPS,), jnp.float32, 0.1, 0.4), 0.1, 0.4)
    step_index = jax.random.randint(key_list[6], (1,), 0, STEPS).astype(jnp.int32)
    embed_weight = normal_values(key_list[7], (CHAN, D), CHAN ** -0.5, 0.75, (), jnp.float32)
    block_mod = normal_values(key_list[8], (2, 2, D), 0.5, 3.0, ((0, 2),), jnp.float32)
    qkv_weight = normal_values(key_list[9], (D, 3, D), D ** -0.5, 0.109375, ((2, 8),))
    qk_gains = jnp.clip(1.0 + 0.15 * jax.random.normal(key_list[10], (2, HEAD_DIM), jnp.float32), 0.25, 1.75)
    return dict(hidden=hidden, final_mod=final_mod, final_weight=final_weight, latent=latent, guidance=guidance, step_size=step_size, step_index=step_index, embed_weight=embed_weight, block_mod=block_mod, qkv_weight=qkv_weight, qk_gains=qk_gains)


def layer_norm(rows):
    mean = lax.optimization_barrier(jnp.mean(rows, axis=-1, keepdims=True))
    centred = rows - mean
    var = lax.optimization_barrier(jnp.mean(centred * centred, axis=-1, keepdims=True))
    return centred * lax.rsqrt(var + 1e-06)

def modulate(rows, mod):
    return layer_norm(rows) * (1.0 + mod[1]) + mod[0]

def rms_scale(values, gain):
    power = lax.optimization_barrier(jnp.mean(values * values, axis=-1, keepdims=True))
    return values * lax.rsqrt(power + 1e-06) * gain

def axis_angles(coord, width):
    exponents = jnp.arange(0, width, 2).astype(jnp.float32) / width
    freqs = 1.0 / 256.0 ** exponents
    return coord.astype(jnp.float32)[:, None] * freqs[None, :]

def rope_angles(positions):
    time_dim = HEAD_DIM // 8
    space_dim = (HEAD_DIM - time_dim) // 2
    frame = positions // (GRID_H * GRID_W)
    row_pos = positions // GRID_W % GRID_H
    col_pos = positions % GRID_W
    return jnp.concatenate([axis_angles(frame, time_dim), axis_angles(row_pos, space_dim), axis_angles(col_pos, space_dim)], axis=-1)

def apply_rope(values, angles):
    count, heads, width = values.shape
    pairs = values.reshape(count, heads, width // 2, 2)
    first = pairs[..., 0]
    second = pairs[..., 1]
    cosine = jnp.cos(angles)[:, None, :]
    sine = jnp.sin(angles)[:, None, :]
    rotated = jnp.stack([first * cosine - second * sine, first * sine + second * cosine], axis=-1)
    return rotated.reshape(count, heads, width)

def project_heads(normed, qkv_weight, qk_gains, angles):
    mixed = jnp.einsum('rd,dtc->rtc', normed.astype(jnp.float32), qkv_weight.astype(jnp.float32))
    count = mixed.shape[0]
    split = mixed.reshape(count, 3, HEADS, HEAD_DIM)
    query = apply_rope(rms_scale(split[:, 0], qk_gains[0]), angles).astype(jnp.bfloat16)
    key_part = apply_rope(rms_scale(split[:, 1], qk_gains[1]), angles).astype(jnp.bfloat16)
    value = split[:, 2].astype(jnp.bfloat16)
    return (query, key_part, value)

def attend_heads(query, key_part, value):
    scale = HEAD_DIM ** (-0.5)

    def single(args):
        q_head, k_head, v_head = args
        scores = jnp.dot(q_head, k_head.T, preferred_element_type=jnp.float32) * scale
        weights = jnp.exp(scores)
        total = lax.optimization_barrier(jnp.sum(weights, axis=-1, keepdims=True))
        numer = jnp.dot(weights.astype(jnp.bfloat16), v_head, preferred_element_type=jnp.float32)
        return numer / total
    result = lax.map(single, (jnp.transpose(query, (1, 0, 2)), jnp.transpose(key_part, (1, 0, 2)), jnp.transpose(value, (1, 0, 2))))
    return jnp.transpose(result, (1, 0, 2)).reshape(query.shape[0], HEADS * HEAD_DIM).astype(jnp.bfloat16)

def reference(hidden, final_mod, final_weight, latent, guidance, step_size, step_index, embed_weight, block_mod, qkv_weight, qk_gains):
    chosen = (jnp.arange(STEPS, dtype=jnp.int32) == step_index[0]).astype(jnp.float32)
    scale_now = jnp.sum(chosen * guidance)
    step_now = jnp.sum(chosen * step_size)
    velocities = []
    for branch in range(2):
        final_rows = modulate(hidden[branch].astype(jnp.float32), final_mod[branch]).astype(jnp.bfloat16)
        velocities.append(jnp.dot(final_rows, final_weight, preferred_element_type=jnp.float32))
    guided = velocities[1] + scale_now * (velocities[0] - velocities[1])
    next_latent = latent - step_now * guided
    embedded = jnp.dot(next_latent, embed_weight, precision=lax.Precision.HIGHEST)
    angles = rope_angles(jnp.arange(TOKENS, dtype=jnp.int32))
    outputs = []
    for branch in range(2):
        normed = modulate(embedded, block_mod[branch]).astype(jnp.bfloat16)
        query, key_part, value = project_heads(normed, qkv_weight, qk_gains, angles)
        outputs.append(attend_heads(query, key_part, value))
    return (next_latent, jnp.stack(outputs, axis=0))
```

```python
import functools
import math

import jax
import jax.numpy as jnp
import numpy as np
from jax import lax
from jax.experimental import pallas as pl
from jax.experimental.pallas import tpu as pltpu
from jax.sharding import PartitionSpec as P

HEAD_DIM = 128
GRID_H = 32
GRID_W = 32
CHAN = 64
EPS = 1e-6
MESH = pl.DeviceIdType.MESH
F32 = jnp.float32
BF16 = jnp.bfloat16


def pair_angles():
    time_dim = HEAD_DIM // 8
    space_dim = (HEAD_DIM - time_dim) // 2
    out = []
    for coords, width in ((8, time_dim), (GRID_H, space_dim), (GRID_W, space_dim)):
        freqs = 1.0 / 256.0 ** (np.arange(0, width, 2) / width)
        out.append(np.arange(coords)[:, None] * freqs[None, :])
    return out


def rope_tables():
    time, row, col = pair_angles()
    frames = time.shape[0]
    blocks = GRID_H // 2
    key = np.zeros((64, 2, blocks, GRID_W))
    query = np.zeros((blocks, 64, 2, 2, GRID_W))
    for half in range(2):
        for b in range(blocks):
            key[8:36, half, b] = row[2 * b + half][:, None]
            key[36:64, half, b] = col.T
            query[b, 8:36, :, half] = row[2 * b + half][:, None, None]
            query[b, 36:64, :, half] = col.T[:, None]
    key = key.reshape(64, 2 * blocks * GRID_W)
    query = query.reshape(blocks, 64, 128)
    query_time = np.repeat(time.T, 64, axis=1)
    key_time = np.repeat(time[:, :, None], 128, axis=2)

    def both(angles, axis):
        return np.stack([np.cos(angles), np.sin(angles)], axis=axis).astype(np.float32)

    return both(key, 0), both(key_time, 1), both(query, 1), both(query_time, 0)


def mm(a, b):
    return jnp.dot(a, b, preferred_element_type=F32)


def mm_nt(a, b, precision=None):
    return lax.dot_general(a, b, (((1,), (1,)), ((), ())), precision=precision, preferred_element_type=F32)


def split_bf16(value):
    high = value.astype(BF16)
    return high, (value - high.astype(F32)).astype(BF16)


def kernel(
    n_uly,
    n_blk,
    guid_s,
    size_s,
    index_s,
    hidden_h,
    fmod_h,
    fw_h,
    latent_h,
    embed_h,
    bmod_h,
    w_h,
    gains_v,
    ktab_h,
    ktime_h,
    qtab_h,
    qtime_h,
    next_ref,
    out_ref,
    hidden_v,
    fmod_v,
    fw_v,
    latent_v,
    embed_v,
    bmod_v,
    w_v,
    ktab_v,
    ktime_v,
    qtab_v,
    qtime_v,
    vel_mine,
    vel_other,
    xp_v,
    xq_v,
    lhs_v,
    tk_v,
    tq_v,
    sv_v,
    tab_v,
    aug_v,
    kt_v,
    q_v,
    acc_v,
    stage_v,
    load_sem,
    vel_send,
    vel_recv,
    blk_send,
    blk_recv,
    uly_send,
    uly_recv,
    x_send,
    x_recv,
    sib_send,
    sib_recv,
    out_send,
    out_recv,
    own_sem,
):
    cfg = lax.axis_index("cfg")
    uly = lax.axis_index("uly")
    blk = lax.axis_index("blk")
    x_at = uly // 2
    core = uly % 2
    sib = uly + 1 - 2 * core
    n_x = n_uly // 2

    def remote(src, dst, send, recv, device):
        return pltpu.make_async_remote_copy(
            src_ref=src, dst_ref=dst, send_sem=send, recv_sem=recv, device_id=device, device_id_type=MESH
        )

    pairs = [
        (hidden_h, hidden_v),
        (fmod_h, fmod_v),
        (fw_h, fw_v),
        (latent_h, latent_v),
        (embed_h, embed_v),
        (bmod_h, bmod_v),
        (w_h.at[0], w_v.at[0]),
        (w_h.at[1], w_v.at[1]),
        (w_h.at[2], w_v.at[2]),
        (ktab_h, ktab_v),
        (ktime_h, ktime_v),
        (qtab_h.at[blk], qtab_v),
        (qtime_h, qtime_v),
    ]
    loads = [pltpu.make_async_copy(s, d, load_sem.at[i]) for i, (s, d) in enumerate(pairs)]
    for load in loads:
        load.start()

    barrier = pltpu.get_barrier_semaphore()
    pl.semaphore_signal(barrier, inc=1, device_id=(1 - cfg, uly, blk), device_id_type=MESH)
    for d in range(1, n_blk):
        pl.semaphore_signal(barrier, inc=1, device_id=(cfg, uly, (blk + d) % n_blk), device_id_type=MESH)
    for d in range(1, n_uly):
        pl.semaphore_signal(barrier, inc=1, device_id=(cfg, (uly + d) % n_uly, blk), device_id_type=MESH)

    for i in range(3):
        loads[i].wait()
    rows = hidden_v[...].astype(F32)
    mean = jnp.mean(rows, axis=1, keepdims=True)
    rows = rows - mean
    var = jnp.mean(rows * rows, axis=1, keepdims=True)
    rows = rows * lax.rsqrt(var + EPS)
    rows = (rows * (1.0 + fmod_v[1:2, :]) + fmod_v[0:1, :]).astype(BF16)
    vel = mm_nt(rows, fw_v[...])
    vel_mine[...] = jnp.concatenate([vel[0:32], vel[32:64]], axis=1)
    pl.semaphore_wait(barrier, n_blk + n_uly - 1)
    vel_copy = remote(vel_mine, vel_other, vel_send, vel_recv, (1 - cfg, uly, blk))
    vel_copy.start()

    loads[3].wait()
    loads[4].wait()
    loads[5].wait()
    emb = embed_v[...]
    emb = emb - jnp.mean(emb, axis=1, keepdims=True)
    high, low = split_bf16(emb)
    stack = jnp.concatenate([high, low], axis=0)
    gram = mm_nt(stack, stack)
    gram = (gram[0:64, 0:64] + gram[0:64, 64:128] + gram[64:128, 0:64] + gram[64:128, 64:128]) * (1.0 / emb.shape[1])
    high, low = split_bf16(emb * (1.0 + bmod_v[1:2, :]))
    lhs_v[0:64, :] = high
    lhs_v[64:128, :] = low
    high, low = split_bf16(bmod_v[0:1, :])
    lhs_v[128:144, :] = jnp.concatenate([high, low, jnp.zeros((14, high.shape[1]), BF16)], axis=0)

    step = index_s[0]
    scale_now = guid_s[step]
    step_now = size_s[step]
    vel_copy.wait()
    mine = vel_mine[...]
    other = vel_other[...]
    cond = jnp.where(cfg == 0, mine, other)
    uncond = jnp.where(cfg == 0, other, mine)
    guided = uncond + scale_now * (cond - uncond)
    guided = jnp.concatenate([guided[:, 0:64], guided[:, 64:128]], axis=0)
    latent = latent_v[...] - step_now * guided
    next_ref[...] = latent
    power = jnp.dot(latent, gram, precision=lax.Precision.HIGHEST, preferred_element_type=F32)
    var = jnp.maximum(jnp.sum(power * latent, axis=1, keepdims=True), 0.0)
    normed = (latent * lax.rsqrt(var + EPS)).astype(BF16)
    packed = jnp.concatenate([normed[0:32], normed[32:64]], axis=1)
    own_rows = pl.ds(pl.multiple_of(blk * 32, 32), 32)
    xp_v[uly, own_rows, :] = packed
    xq_v[uly] = packed

    blk_copies = []
    for d in range(1, n_blk):
        there = xp_v.at[uly, own_rows, :]
        blk_copies.append(
            remote(there, there, blk_send.at[d - 1], blk_recv.at[d - 1], (cfg, uly, (blk + d) % n_blk))
        )
    uly_copies = []
    for d in range(1, n_uly):
        there = xq_v.at[uly]
        uly_copies.append(
            remote(there, there, uly_send.at[d - 1], uly_recv.at[d - 1], (cfg, (uly + d) % n_uly, blk))
        )
    for copy in blk_copies + uly_copies:
        copy.start()

    lanes = lax.broadcasted_iota(jnp.int32, (128, 128), 1)
    sublanes = lax.broadcasted_iota(jnp.int32, (128, 128), 0)
    source = jnp.where(sublanes < 64, 2 * sublanes, 2 * sublanes - 127)
    perm = jnp.where(lanes == source, 1.0, 0.0)
    perm_b = perm.astype(BF16)
    lhs = lhs_v[...]
    for j in range(3):
        loads[6 + j].wait()
        full = mm(lhs, w_v[j])
        weight = full[0:64] + full[64:128]
        bias = full[128:129] + full[129:130]
        square = jnp.concatenate([weight, bias, jnp.zeros((63, weight.shape[1]), F32)], axis=0)
        high, low = split_bf16(square)
        for h in range(3):
            cols = slice(h * 128, h * 128 + 128)
            if j == 2:
                sv_v[h, 0:128, :] = high[:, cols]
                sv_v[h, 128:256, :] = low[:, cols]
            else:
                target = tq_v if j == 0 else tk_v
                target[cols, 0:128] = mm_nt(perm_b, high[:, cols]).astype(BF16)
                target[cols, 128:256] = mm_nt(perm_b, low[:, cols]).astype(BF16)

    for i in range(9, 13):
        loads[i].wait()
    gains = jnp.concatenate([gains_v[...], jnp.zeros((6, 128), F32)], axis=0)
    gains = mm_nt(perm, gains, precision=lax.Precision.HIGHEST)
    ga_q = gains[0:64, 0:1] * (math.log2(math.e) / math.sqrt(HEAD_DIM))
    gb_q = gains[64:128, 0:1] * (math.log2(math.e) / math.sqrt(HEAD_DIM))
    ga_k = gains[0:64, 1:2]
    gb_k = gains[64:128, 1:2]
    cosine, sine = ktab_v[0], ktab_v[1]
    tab_v[0] = ga_k * cosine
    tab_v[1] = gb_k * sine
    tab_v[2] = ga_k * sine
    tab_v[3] = gb_k * cosine
    ga_t = jnp.broadcast_to(ga_k[0:8], (8, 128))
    gb_t = jnp.broadcast_to(gb_k[0:8], (8, 128))

    one_hot = jnp.where(lax.broadcasted_iota(jnp.int32, (1, 128), 1) == 64, 1.0, 0.0)
    low_lanes = lax.broadcasted_iota(jnp.int32, (1, 128), 1) < 64

    def unpack(value):
        wide = value.astype(F32)
        first = jnp.where(low_lanes, wide, one_hot).astype(BF16)
        second = jnp.where(low_lanes, pltpu.roll(wide, 64, 1), one_hot).astype(BF16)
        return first, second

    def rotate(proj, t1, t2, t3, t4):
        a, b = proj[0:64], proj[64:128]
        power = jnp.sum(a * a + b * b, axis=0, keepdims=True) * (1.0 / HEAD_DIM)
        scale = lax.rsqrt(power + EPS)
        return (a * t1 - b * t2) * scale, (a * t3 + b * t4) * scale

    def make_keys(chunk, slot):
        cos_t, sin_t = ktime_v[chunk, 0], ktime_v[chunk, 1]
        for i, row in enumerate((ga_t * cos_t, gb_t * sin_t, ga_t * sin_t, gb_t * cos_t)):
            tab_v[i, 0:8, :] = jnp.concatenate([row] * 8, axis=1)
        halves = unpack(xp_v[chunk])
        for half in range(2):
            cols = slice(half * 512, half * 512 + 512)
            aug_v[slot, cols, :] = halves[half]
            proj = mm_nt(tk_v[...], jnp.concatenate([halves[half]] * 2, axis=1))
            tabs = [tab_v[i, :, cols] for i in range(4)]
            for h in range(3):
                ka, kb = rotate(proj[h * 128 : h * 128 + 128], *tabs)
                kt_v[slot, h, 0:64, cols] = ka.astype(BF16)
                kt_v[slot, h, 64:128, cols] = kb.astype(BF16)

    def blk_from(d):
        there = xp_v.at[uly, pl.ds(pl.multiple_of((blk + n_blk - d) % n_blk * 32, 32), 32), :]
        return remote(there, there, blk_send.at[d - 1], blk_recv.at[d - 1], (cfg, uly, (blk + d) % n_blk))

    for d in range(1, n_blk):
        blk_from(d).wait_recv()

    def x_copy(d, slot):
        there = xp_v.at[slot]
        return remote(there, there, x_send.at[d - 1], x_recv.at[d - 1], (cfg, (x_at + d) % n_x * 2 + core, blk))

    def sib_copy(d, slot):
        there = xp_v.at[slot]
        return remote(there, there, sib_send.at[d], sib_recv.at[d], (cfg, sib, blk))

    def x_slot(d):
        return (x_at + n_x - d) % n_x * 2 + core

    def x_slot_sib(d):
        return (x_at + n_x - d) % n_x * 2 + 1 - core

    for d in (1, 3, 2):
        x_copy(d, uly).start()
    sib_copy(0, uly).start()

    for d in range(1, n_uly):
        there = xq_v.at[(uly + n_uly - d) % n_uly]
        remote(there, there, uly_send.at[d - 1], uly_recv.at[d - 1], (cfg, uly, blk)).wait_recv()
    parts = []
    for u in range(n_uly):
        parts += list(unpack(xq_v[u]))
    rows_q = jnp.concatenate(parts, axis=0)
    proj = mm_nt(tq_v[...], jnp.concatenate([rows_q, rows_q], axis=1))
    cos_q = jnp.concatenate([qtime_v[0], jnp.concatenate([qtab_v[0, 8:64]] * 4, axis=1)], axis=0)
    sin_q = jnp.concatenate([qtime_v[1], jnp.concatenate([qtab_v[1, 8:64]] * 4, axis=1)], axis=0)
    tabs = (ga_q * cos_q, gb_q * sin_q, ga_q * sin_q, gb_q * cos_q)
    for h in range(3):
        qa, qb = rotate(proj[h * 128 : h * 128 + 128], *tabs)
        q_v[h] = jnp.transpose(jnp.concatenate([qa, qb], axis=0)).astype(BF16)

    make_keys(uly, 0)
    acc_v[...] = jnp.zeros_like(acc_v)

    def attend(h, slot):
        scores = mm(q_v[h], kt_v[slot, h])
        return mm(jnp.exp2(scores).astype(BF16), aug_v[slot])

    def frame_of(r):
        d = jnp.where(r < 2, 0, jnp.where(r >= 6, 2, jnp.where(r % 2 == 0, 1, 3)))
        other = jnp.where(r < 4, jnp.where(r == 1, 1, 0), jnp.where(r < 6, 1, r % 2))
        at = (x_at + n_x - d) % n_x
        return at * 2 + jnp.where(other == 1, 1 - core, core)

    def body(r, _):
        slot = r % 2

        @pl.when(r == 0)
        def _():
            sib_copy(0, sib).wait_recv()

        @pl.when(r == 1)
        def _():
            x_copy(1, x_slot(1)).wait_recv()
            sib_copy(1, x_slot(1)).start()

        @pl.when(r == 2)
        def _():
            x_copy(3, x_slot(3)).wait_recv()
            sib_copy(3, x_slot(3)).start()

        @pl.when(r == 3)
        def _():
            sib_copy(1, x_slot_sib(1)).wait_recv()

        @pl.when(r == 4)
        def _():
            sib_copy(3, x_slot_sib(3)).wait_recv()
            x_copy(2, x_slot(2)).wait_recv()
            sib_copy(2, x_slot(2)).start()

        @pl.when(r == 6)
        def _():
            sib_copy(2, x_slot_sib(2)).wait_recv()

        make_keys(frame_of(r + 1), 1 - slot)
        for h in range(3):
            acc_v[h] += attend(h, slot)
        return 0

    lax.fori_loop(0, n_uly - 1, body, 0)

    def out_copy(h, d):
        to = (uly + d) % n_uly
        src = stage_v.at[h, pl.ds(pl.multiple_of(to * 64, 64), 64), :]
        dst = out_ref.at[:, pl.ds(pl.multiple_of((uly * 3 + h) * 128, 128), 128)]
        return remote(src, dst, out_send.at[h, d - 1], out_recv.at[h, d - 1], (cfg, to, blk))

    def out_from(h, d):
        source = (uly + n_uly - d) % n_uly
        src = stage_v.at[h, pl.ds(pl.multiple_of(uly * 64, 64), 64), :]
        dst = out_ref.at[:, pl.ds(pl.multiple_of((source * 3 + h) * 128, 128), 128)]
        return remote(src, dst, out_send.at[h, d - 1], out_recv.at[h, d - 1], (cfg, source, blk))

    def own_copy(h):
        src = stage_v.at[h, pl.ds(pl.multiple_of(uly * 64, 64), 64), :]
        dst = out_ref.at[:, pl.ds(pl.multiple_of((uly * 3 + h) * 128, 128), 128)]
        return pltpu.make_async_copy(src, dst, own_sem.at[h])

    for h in range(3):
        numer = acc_v[h] + attend(h, (n_uly - 1) % 2)
        mean_x = numer / numer[:, 64:65]
        high, low = split_bf16(mean_x)
        result = mm(jnp.concatenate([high, high], axis=1), sv_v[h]) + mm(low, sv_v[h, 0:128])
        stage_v[h] = result.astype(BF16)
        for d in range(1, n_uly):
            out_copy(h, d).start()
        own_copy(h).start()

    vel_done = []
    for copy in blk_copies + uly_copies:
        copy.wait_send()
    for d in range(1, n_x):
        x_copy(d, uly).wait_send()
    sib_copy(0, uly).wait_send()
    for d in range(1, n_x):
        sib_copy(d, x_slot(d)).wait_send()
    for h in range(3):
        own_copy(h).wait()
        for d in range(1, n_uly):
            out_copy(h, d).wait_send()
            out_from(h, d).wait_recv()


def solution(mesh):
    n_uly = mesh.shape["uly"]
    n_blk = mesh.shape["blk"]
    tables = rope_tables()

    def on_device(
        hidden, final_mod, final_weight, latent, guidance, step_size, step_index, embed_weight, block_mod, qkv_weight, qk_gains
    ):
        smem = pl.BlockSpec(memory_space=pltpu.SMEM)
        vmem = pl.BlockSpec(memory_space=pltpu.VMEM)
        anywhere = pl.BlockSpec(memory_space=pl.ANY)
        rows, width = hidden.shape[1:]
        cols = qkv_weight.shape[2]
        heads = cols // HEAD_DIM
        keys = GRID_H * GRID_W
        queries = rows * n_uly
        dma = pltpu.SemaphoreType.DMA
        next_latent, attention = pl.pallas_call(
            functools.partial(kernel, n_uly, n_blk),
            out_shape=(
                jax.ShapeDtypeStruct((rows, CHAN), F32),
                jax.ShapeDtypeStruct((rows, width), BF16),
            ),
            in_specs=[smem] * 3 + [anywhere] * 7 + [vmem] + [anywhere] * 4,
            out_specs=(vmem, anywhere),
            scratch_shapes=[
                pltpu.VMEM((rows, width), BF16),
                pltpu.VMEM((2, width), F32),
                pltpu.VMEM((CHAN, width), BF16),
                pltpu.VMEM((rows, CHAN), F32),
                pltpu.VMEM((CHAN, width), F32),
                pltpu.VMEM((2, width), F32),
                pltpu.VMEM((3, width, cols), BF16),
                pltpu.VMEM(tables[0].shape, F32),
                pltpu.VMEM(tables[1].shape, F32),
                pltpu.VMEM(tables[2].shape[1:], F32),
                pltpu.VMEM(tables[3].shape, F32),
                pltpu.VMEM((32, 128), F32),
                pltpu.VMEM((32, 128), F32),
                pltpu.VMEM((n_uly, n_blk * 32, 128), BF16),
                pltpu.VMEM((n_uly, 32, 128), BF16),
                pltpu.VMEM((144, width), BF16),
                pltpu.VMEM((cols, 256), BF16),
                pltpu.VMEM((cols, 256), BF16),
                pltpu.VMEM((heads, 256, 128), BF16),
                pltpu.VMEM((4, 64, keys), F32),
                pltpu.VMEM((2, keys, 128), BF16),
                pltpu.VMEM((2, heads, 128, keys), BF16),
                pltpu.VMEM((heads, queries, 128), BF16),
                pltpu.VMEM((heads, queries, 128), F32),
                pltpu.VMEM((heads, queries, 128), BF16),
                dma((13,)),
                dma,
                dma,
                dma((n_blk - 1,)),
                dma((n_blk - 1,)),
                dma((n_uly - 1,)),
                dma((n_uly - 1,)),
                dma((n_uly // 2 - 1,)),
                dma((n_uly // 2 - 1,)),
                dma((n_uly // 2,)),
                dma((n_uly // 2,)),
                dma((heads, n_uly - 1)),
                dma((heads, n_uly - 1)),
                dma((heads,)),
            ],
            compiler_params=pltpu.CompilerParams(
                collective_id=0, has_side_effects=True, vmem_limit_bytes=56 << 20
            ),
        )(
            guidance,
            step_size,
            step_index,
            hidden[0],
            final_mod[0],
            final_weight.T,
            latent,
            embed_weight,
            block_mod[0],
            jnp.transpose(qkv_weight, (1, 0, 2)),
            qk_gains,
            *[jnp.asarray(t) for t in tables],
        )
        return (next_latent, attention[None])

    return jax.shard_map(
        on_device,
        mesh=mesh,
        in_specs=(
            P("cfg", ("uly", "blk"), None),
            P("cfg", None, None),
            P(),
            P(("uly", "blk"), None),
            P(),
            P(),
            P(),
            P(),
            P("cfg", None, None),
            P(None, None, "uly"),
            P(),
        ),
        out_specs=(P(("uly", "blk"), None), P("cfg", ("uly", "blk"), None)),
        check_vma=False,
    )
```

```python
import functools
import math

import jax
import jax.numpy as jnp
import numpy as np
from jax import lax
from jax.experimental import pallas as pl
from jax.experimental.pallas import tpu as pltpu
from jax.sharding import PartitionSpec as P

HEAD_DIM = 128
GRID_H = 32
GRID_W = 32
CHAN = 64
EPS = 1e-6
MESH = pl.DeviceIdType.MESH
F32 = jnp.float32
BF16 = jnp.bfloat16


def pair_angles():
    time_dim = HEAD_DIM // 8
    space_dim = (HEAD_DIM - time_dim) // 2
    out = []
    for coords, width in ((8, time_dim), (GRID_H, space_dim), (GRID_W, space_dim)):
        freqs = 1.0 / 256.0 ** (np.arange(0, width, 2) / width)
        out.append(np.arange(coords)[:, None] * freqs[None, :])
    return out


def rope_tables(n_uly, n_y, n_z):
    time, row, col = pair_angles()
    n_x = n_uly // 2
    key = np.zeros((n_z, 2, 64, 2, n_y, GRID_W))
    query = np.zeros((n_y * n_z, 64, 2, 2, GRID_W))
    for half in range(2):
        for y in range(n_y):
            for z in range(n_z):
                at = row[2 * (y * n_z + z) + half]
                key[z, half, 8:36, :, y] = at[:, None, None]
                key[z, half, 36:64, :, y] = col.T[:, None]
                query[y * n_z + z, 8:36, :, half] = at[:, None, None]
                query[y * n_z + z, 36:64, :, half] = col.T[:, None]
    key = key.reshape(n_z, 2, 64, 128)
    query = query.reshape(n_y * n_z, 64, 128)
    frame = [2 * x + core for core in range(2) for x in range(n_x)]
    key_time = np.repeat(time[frame].T, n_y * GRID_W, axis=1)
    query_time = np.repeat(time.T, 2 * GRID_W, axis=1)

    def both(angles, axis):
        return np.stack([np.cos(angles), np.sin(angles)], axis=axis).astype(np.float32)

    return both(key, 2), both(key_time, 0), both(query, 1), both(query_time, 0)


def mm(a, b):
    return jnp.dot(a, b, preferred_element_type=F32)


def mm_nt(a, b, precision=None):
    return lax.dot_general(a, b, (((1,), (1,)), ((), ())), precision=precision, preferred_element_type=F32)


def split_bf16(value):
    high = value.astype(BF16)
    return high, (value - high.astype(F32)).astype(BF16)


def kernel(
    n_uly,
    n_y,
    n_z,
    guid_s,
    size_s,
    index_s,
    hidden_h,
    fmod_h,
    fw_h,
    latent_h,
    embed_h,
    bmod_h,
    w_h,
    gains_v,
    ktab_h,
    ktime_h,
    qtab_h,
    qtime_h,
    next_ref,
    out_ref,
    hidden_v,
    fmod_v,
    fw_v,
    latent_v,
    embed_v,
    bmod_v,
    w_v,
    ktab_v,
    ktime_v,
    qtab_v,
    qtime_v,
    vel_mine,
    vel_other,
    xp_v,
    lhs_v,
    tk_v,
    tq_v,
    sv_v,
    aug_v,
    kt_v,
    q_v,
    acc_v,
    stage_v,
    load_sem,
    vel_send,
    vel_recv,
    plane_send,
    plane_recv,
    z_send,
    z_recv,
    group_send,
    group_recv,
    sib_send,
    sib_recv,
    out_send,
    out_recv,
    own_sem,
):
    cfg = lax.axis_index("cfg")
    uly = lax.axis_index("uly")
    blk = lax.axis_index("blk")
    x_at = uly // 2
    core = uly % 2
    sib = uly + 1 - 2 * core
    y_at = blk // n_z
    z_at = blk % n_z
    n_x = n_uly // 2
    half_rows = n_x * n_y * 32

    def remote(src, dst, send, recv, device):
        return pltpu.make_async_remote_copy(
            src_ref=src, dst_ref=dst, send_sem=send, recv_sem=recv, device_id=device, device_id_type=MESH
        )

    def near(dx, dy, dc):
        return (cfg, (x_at + dx) % n_x * 2 + (core + dc) % 2, (y_at + dy) % n_y * n_z + z_at)

    def ahead(off):
        return (cfg, uly, y_at * n_z + (z_at + n_z + off) % n_z)

    plane = [(dx, dy, dc) for dx in (2, 1, 3, 0) for dy in (1, 0) for dc in (1, 0) if dx + dy + dc > 0]
    side = [(dx, dy, 0) for dx in (2, 1, 3, 0) for dy in (1, 0) if dx + dy > 0]
    groups = [(1, 2), (3, n_z - 1)]
    leave = (2, 1, 3, 0)

    pairs = [
        (hidden_h, hidden_v),
        (fmod_h, fmod_v),
        (fw_h, fw_v),
        (latent_h, latent_v),
        (embed_h, embed_v),
        (bmod_h, bmod_v),
        (w_h.at[0], w_v.at[0]),
        (w_h.at[1], w_v.at[1]),
        (w_h.at[2], w_v.at[2]),
        (ktab_h, ktab_v),
        (ktime_h, ktime_v),
        (qtab_h.at[blk], qtab_v),
        (qtime_h, qtime_v),
    ]
    loads = [pltpu.make_async_copy(s, d, load_sem.at[i]) for i, (s, d) in enumerate(pairs)]
    for load in loads[:4]:
        load.start()

    barrier = pltpu.get_barrier_semaphore()
    for off in range(1, n_z):
        pl.semaphore_signal(barrier, inc=1, device_id=ahead(off), device_id_type=MESH)
    for offs in plane:
        pl.semaphore_signal(barrier, inc=1, device_id=near(*offs), device_id_type=MESH)
    pl.semaphore_signal(barrier, inc=1, device_id=(1 - cfg, uly, blk), device_id_type=MESH)

    for i in range(3):
        loads[i].wait()
    for load in loads[4:]:
        load.start()
    rows = hidden_v[...].astype(F32)
    mean = jnp.mean(rows, axis=1, keepdims=True)
    rows = rows - mean
    var = jnp.mean(rows * rows, axis=1, keepdims=True)
    rows = rows * lax.rsqrt(var + EPS)
    rows = (rows * (1.0 + fmod_v[1:2, :]) + fmod_v[0:1, :]).astype(BF16)
    vel = mm_nt(rows, fw_v[...])
    vel_mine[...] = jnp.concatenate([vel[0:32], vel[32:64]], axis=1)

    pl.semaphore_wait(barrier, len(plane) + n_z)
    vel_copy = remote(vel_mine, vel_other, vel_send, vel_recv, (1 - cfg, uly, blk))
    vel_copy.start()

    loads[3].wait()
    loads[4].wait()
    loads[5].wait()
    emb = embed_v[...]
    emb = emb - jnp.mean(emb, axis=1, keepdims=True)
    high, low = split_bf16(emb)
    stack = jnp.concatenate([high, low], axis=0)
    gram = mm_nt(stack, stack)
    gram = (gram[0:64, 0:64] + gram[0:64, 64:128] + gram[64:128, 0:64] + gram[64:128, 64:128]) * (1.0 / emb.shape[1])
    high, low = split_bf16(emb * (1.0 + bmod_v[1:2, :]))
    lhs_v[0:64, :] = high
    lhs_v[64:128, :] = low
    high, low = split_bf16(bmod_v[0:1, :])
    lhs_v[128:144, :] = jnp.concatenate([high, low, jnp.zeros((14, high.shape[1]), BF16)], axis=0)

    step = index_s[0]
    scale_now = guid_s[step]
    step_now = size_s[step]
    vel_copy.wait()
    mine = vel_mine[...]
    other = vel_other[...]
    cond = jnp.where(cfg == 0, mine, other)
    uncond = jnp.where(cfg == 0, other, mine)
    guided = uncond + scale_now * (cond - uncond)
    guided = jnp.concatenate([guided[:, 0:64], guided[:, 64:128]], axis=0)
    latent = latent_v[...] - step_now * guided
    next_ref[...] = latent
    power = jnp.dot(latent, gram, precision=lax.Precision.HIGHEST, preferred_element_type=F32)
    var = jnp.maximum(jnp.sum(power * latent, axis=1, keepdims=True), 0.0)
    normed = (latent * lax.rsqrt(var + EPS)).astype(BF16)
    own_at = ((core * n_x + x_at) * n_y + y_at) * 32
    own_rows = pl.ds(pl.multiple_of(own_at, 32), 32)
    own_half = pl.ds(pl.multiple_of(core * half_rows, half_rows), half_rows)
    sib_half = pl.ds(pl.multiple_of((1 - core) * half_rows, half_rows), half_rows)
    xp_v[0, own_rows, :] = jnp.concatenate([normed[0:32], normed[32:64]], axis=1)

    def rows_of(dx, dy, dc):
        at = ((core + dc) % 2 * n_x + (x_at + n_x - dx) % n_x) * n_y + (y_at + dy) % n_y
        return pl.ds(pl.multiple_of(at * 32, 32), 32)

    def offset(r):
        return (r + 1) // 2 * (2 * (r % 2) - 1)

    def z_copy(r):
        src = xp_v.at[0, own_rows, :]
        dst = xp_v.at[r, own_rows, :]
        return remote(src, dst, z_send.at[r - 1], z_recv.at[r - 1], ahead(-offset(r)))

    def plane_copy(k):
        there = xp_v.at[0, own_rows, :]
        return remote(there, there, plane_send.at[k], plane_recv.at[k], near(*plane[k]))

    def plane_from(k):
        there = xp_v.at[0, rows_of(*plane[k]), :]
        return remote(there, there, plane_send.at[k], plane_recv.at[k], near(*plane[k]))

    def group_copy(g, k):
        first, last = groups[g]
        there = xp_v.at[first : last + 1, own_rows, :]
        return remote(there, there, group_send.at[g, k], group_recv.at[g, k], near(*side[k]))

    def group_from(g, k):
        first, last = groups[g]
        there = xp_v.at[first : last + 1, rows_of(*side[k]), :]
        return remote(there, there, group_send.at[g, k], group_recv.at[g, k], near(*side[k]))

    def sib_copy(g):
        first, last = groups[g]
        there = xp_v.at[first : last + 1, own_half, :]
        return remote(there, there, sib_send.at[g], sib_recv.at[g], (cfg, sib, blk))

    def sib_from(g):
        first, last = groups[g]
        there = xp_v.at[first : last + 1, sib_half, :]
        return remote(there, there, sib_send.at[g], sib_recv.at[g], (cfg, sib, blk))

    def spread(g):
        first, last = groups[g]
        for r in range(first, last + 1):
            z_copy(r).wait_recv()
        for k in range(len(side)):
            group_copy(g, k).start()

    def share(g):
        for k in range(len(side)):
            group_from(g, k).wait_recv()
        sib_copy(g).start()

    for r in range(1, 3):
        z_copy(r).start()
    for k in range(len(plane)):
        plane_copy(k).start()
    for r in range(3, n_z):
        z_copy(r).start()

    lanes = lax.broadcasted_iota(jnp.int32, (128, 128), 1)
    sublanes = lax.broadcasted_iota(jnp.int32, (128, 128), 0)
    source = jnp.where(sublanes < 64, 2 * sublanes, 2 * sublanes - 127)
    perm = jnp.where(lanes == source, 1.0, 0.0)
    perm_b = perm.astype(BF16)
    lhs = lhs_v[...]
    for j in range(3):
        loads[6 + j].wait()
        full = mm(lhs, w_v[j])
        weight = full[0:64] + full[64:128]
        bias = full[128:129] + full[129:130]
        square = jnp.concatenate([weight, bias, jnp.zeros((63, weight.shape[1]), F32)], axis=0)
        high, low = split_bf16(square)
        for h in range(3):
            cols = slice(h * 128, h * 128 + 128)
            if j == 2:
                sv_v[h, 0:128, :] = high[:, cols]
                sv_v[h, 128:256, :] = low[:, cols]
            else:
                target = tq_v if j == 0 else tk_v
                target[cols, 0:128] = mm_nt(perm_b, high[:, cols]).astype(BF16)
                target[cols, 128:256] = mm_nt(perm_b, low[:, cols]).astype(BF16)

    for i in range(9, 13):
        loads[i].wait()
    gains = jnp.concatenate([gains_v[...], jnp.zeros((6, 128), F32)], axis=0)
    gains = mm_nt(perm, gains, precision=lax.Precision.HIGHEST)
    ga_q = gains[0:64, 0:1] * (math.log2(math.e) / math.sqrt(HEAD_DIM))
    gb_q = gains[64:128, 0:1] * (math.log2(math.e) / math.sqrt(HEAD_DIM))
    ga_k = gains[0:64, 1:2]
    gb_k = gains[64:128, 1:2]

    one_hot = jnp.where(lax.broadcasted_iota(jnp.int32, (1, 128), 1) == 64, 1.0, 0.0)
    low_lanes = lax.broadcasted_iota(jnp.int32, (1, 128), 1) < 64

    def unpack(value):
        wide = value.astype(F32)
        first = jnp.where(low_lanes, wide, one_hot).astype(BF16)
        second = jnp.where(low_lanes, pltpu.roll(wide, 64, 1), one_hot).astype(BF16)
        return first, second

    def rope_tabs(ga, gb, cosine, sine):
        return ga * cosine, gb * sine, ga * sine, gb * cosine

    def rotate(proj, t1, t2, t3, t4):
        a, b = proj[0:64], proj[64:128]
        power = jnp.sum(a * a + b * b, axis=0, keepdims=True) * (1.0 / HEAD_DIM)
        scale = lax.rsqrt(power + EPS)
        return (a * t1 - b * t2) * scale, (a * t3 + b * t4) * scale

    def laid(time, rest, times):
        return jnp.concatenate([time, jnp.concatenate([rest] * times, axis=1)], axis=0)

    def make_keys(r):
        halves = unpack(xp_v[r])
        at = (z_at + n_z + offset(r)) % n_z
        size = 2 * half_rows
        times = rope_tabs(ga_k[0:8], gb_k[0:8], ktime_v[0], ktime_v[1])
        for half in range(2):
            cols = slice(half * size, half * size + size)
            aug_v[r, cols, :] = halves[half]
            proj = mm_nt(tk_v[...], jnp.concatenate([halves[half]] * 2, axis=1))
            rests = rope_tabs(ga_k[8:64], gb_k[8:64], ktab_v[at, half, 0, 8:64], ktab_v[at, half, 1, 8:64])
            tabs = [laid(t, r, size // 128) for t, r in zip(times, rests)]
            for h in range(3):
                ka, kb = rotate(proj[h * 128 : h * 128 + 128], *tabs)
                kt_v[r, h, 0:64, cols] = ka.astype(BF16)
                kt_v[r, h, 64:128, cols] = kb.astype(BF16)

    def attend(h, r, rows=slice(None)):
        scores = mm(q_v[h, rows], kt_v[r, h])
        return mm(jnp.exp2(scores).astype(BF16), aug_v[r])

    spread(0)
    for k in range(len(plane)):
        plane_from(k).wait_recv()

    parts = []
    for dx in leave:
        for c in range(2):
            at = (c * n_x + (x_at + dx) % n_x) * n_y + y_at
            parts += list(unpack(xp_v[0, pl.ds(pl.multiple_of(at * 32, 32), 32), :]))
    rows_q = jnp.concatenate(parts, axis=0)
    proj = mm_nt(tq_v[...], jnp.concatenate([rows_q, rows_q], axis=1))
    here = [pl.ds(pl.multiple_of((x_at + dx) % n_x * 128, 128), 128) for dx in leave]
    cos_t, sin_t = [jnp.concatenate([qtime_v[i, :, lanes] for lanes in here], axis=1) for i in range(2)]
    times = rope_tabs(ga_q[0:8], gb_q[0:8], cos_t, sin_t)
    rests = rope_tabs(ga_q[8:64], gb_q[8:64], qtab_v[0, 8:64], qtab_v[1, 8:64])
    tabs = [laid(t, r, n_uly * 64 // 128) for t, r in zip(times, rests)]
    for h in range(3):
        qa, qb = rotate(proj[h * 128 : h * 128 + 128], *tabs)
        q_v[h] = jnp.transpose(jnp.concatenate([qa, qb], axis=0)).astype(BF16)

    make_keys(0)
    acc_v[0] = attend(0, 0)
    spread(1)
    acc_v[1] = attend(1, 0)
    share(0)
    acc_v[2] = attend(2, 0)
    sib_from(0).wait_recv()

    make_keys(1)
    for h in range(2):
        acc_v[h] += attend(h, 1)
    share(1)
    make_keys(2)
    acc_v[2] += attend(2, 1)
    for h in range(3):
        acc_v[h] += attend(h, 2)
    sib_from(1).wait_recv()
    make_keys(3)
    for h in range(3):
        acc_v[h] += attend(h, 3)
    for r in range(4, n_z):
        make_keys(r)

    width = 3 * HEAD_DIM

    def out_copy(j, dc, h=None):
        c = (core + dc) % 2
        rows = pl.ds(pl.multiple_of(j * 128 + c * 64, 64), 64)
        first, size = (0, width) if h is None else (h * 128, 128)
        src = stage_v.at[rows, first : first + size]
        dst = out_ref.at[:, pl.ds(pl.multiple_of(uly * width + first, 128), size)]
        if leave[j] + dc == 0:
            return pltpu.make_async_copy(src, dst, own_sem)
        to = (x_at + leave[j]) % n_x * 2 + c
        sem = (h or 0, j, dc)
        return remote(src, dst, out_send.at[sem], out_recv.at[sem], (cfg, to, blk))

    def out_from(j, dc, h=None):
        source = (x_at + n_x - leave[j]) % n_x * 2 + (core + dc) % 2
        first, size = (0, width) if h is None else (h * 128, 128)
        src = stage_v.at[0:64, first : first + size]
        dst = out_ref.at[:, pl.ds(pl.multiple_of(source * width + first, 128), size)]
        sem = (h or 0, j, dc)
        return remote(src, dst, out_send.at[sem], out_recv.at[sem], (cfg, source, blk))

    sends = [(0, 0, None), (0, 1, None), (1, 0, None), (1, 1, None)]
    sends += [(2, dc, h) for h in range(3) for dc in range(2)] + [(3, 1, None)]
    for half in range(2):
        rows = slice(half * 256, half * 256 + 256)
        for h in range(3):
            numer = acc_v[h, rows]
            for r in range(4, n_z):
                numer += attend(h, r, rows)
            mean_x = numer / numer[:, 64:65]
            high, low = split_bf16(mean_x)
            result = mm(jnp.concatenate([high, high], axis=1), sv_v[h]) + mm(low, sv_v[h, 0:128])
            stage_v[rows, h * 128 : h * 128 + 128] = result.astype(BF16)
            if half == 1:
                for dc in (1, 0):
                    out_copy(2, dc, h).start()
        for j in ((0, 1), (3,))[half]:
            for dc in (1, 0):
                out_copy(j, dc).start()

    for k in range(len(plane)):
        plane_copy(k).wait_send()
    for r in range(1, n_z):
        z_copy(r).wait_send()
    for g in range(len(groups)):
        for k in range(len(side)):
            group_copy(g, k).wait_send()
        sib_copy(g).wait_send()
    out_copy(3, 0).wait()
    for j, dc, h in sends:
        out_copy(j, dc, h).wait_send()
        out_from(j, dc, h).wait_recv()


def hand_over(next_in, out_in, next_ref, out_ref):
    next_ref[...] = next_in[...]
    out_ref[...] = out_in[...]


def solution(mesh):
    n_uly = mesh.shape["uly"]
    n_blk = mesh.shape["blk"]
    n_y = 2
    n_z = n_blk // n_y
    tables = rope_tables(n_uly, n_y, n_z)

    def on_device(
        hidden, final_mod, final_weight, latent, guidance, step_size, step_index, embed_weight, block_mod, qkv_weight, qk_gains
    ):
        smem = pl.BlockSpec(memory_space=pltpu.SMEM)
        vmem = pl.BlockSpec(memory_space=pltpu.VMEM)
        anywhere = pl.BlockSpec(memory_space=pl.ANY)
        rows, width = hidden.shape[1:]
        cols = qkv_weight.shape[2]
        heads = cols // HEAD_DIM
        keys = 64 * n_uly * n_y
        queries = rows * n_uly
        dma = pltpu.SemaphoreType.DMA
        next_latent, attention = pl.pallas_call(
            functools.partial(kernel, n_uly, n_y, n_z),
            out_shape=(
                jax.ShapeDtypeStruct((rows, CHAN), F32),
                jax.ShapeDtypeStruct((rows, width), BF16),
            ),
            in_specs=[smem] * 3 + [anywhere] * 7 + [vmem] + [anywhere] * 4,
            out_specs=(vmem, anywhere),
            scratch_shapes=[
                pltpu.VMEM((rows, width), BF16),
                pltpu.VMEM((2, width), F32),
                pltpu.VMEM((CHAN, width), BF16),
                pltpu.VMEM((rows, CHAN), F32),
                pltpu.VMEM((CHAN, width), F32),
                pltpu.VMEM((2, width), F32),
                pltpu.VMEM((3, width, cols), BF16),
                pltpu.VMEM(tables[0].shape, F32),
                pltpu.VMEM(tables[1].shape, F32),
                pltpu.VMEM(tables[2].shape[1:], F32),
                pltpu.VMEM(tables[3].shape, F32),
                pltpu.VMEM((32, 128), F32),
                pltpu.VMEM((32, 128), F32),
                pltpu.VMEM((n_z, n_uly * n_y * 32, 128), BF16),
                pltpu.VMEM((144, width), BF16),
                pltpu.VMEM((cols, 256), BF16),
                pltpu.VMEM((cols, 256), BF16),
                pltpu.VMEM((heads, 256, 128), BF16),
                pltpu.VMEM((n_z, keys, 128), BF16),
                pltpu.VMEM((n_z, heads, 128, keys), BF16),
                pltpu.VMEM((heads, queries, 128), BF16),
                pltpu.VMEM((heads, queries, 128), F32),
                pltpu.VMEM((queries, cols), BF16),
                dma((13,)),
                dma,
                dma,
                dma((n_uly * n_y - 1,)),
                dma((n_uly * n_y - 1,)),
                dma((n_z - 1,)),
                dma((n_z - 1,)),
                dma((2, n_uly // 2 * n_y - 1)),
                dma((2, n_uly // 2 * n_y - 1)),
                dma((2,)),
                dma((2,)),
                dma((heads, n_uly // 2, 2)),
                dma((heads, n_uly // 2, 2)),
                dma,
            ],
            compiler_params=pltpu.CompilerParams(
                collective_id=0, has_side_effects=True, vmem_limit_bytes=56 << 20
            ),
        )(
            guidance,
            step_size,
            step_index,
            hidden[0],
            final_mod[0],
            final_weight.T,
            latent,
            embed_weight,
            block_mod[0],
            jnp.transpose(qkv_weight, (1, 0, 2)),
            qk_gains,
            *[jnp.asarray(t) for t in tables],
        )
        next_latent, attention = pl.pallas_call(
            hand_over,
            out_shape=(
                jax.ShapeDtypeStruct((rows, CHAN), F32),
                jax.ShapeDtypeStruct((rows, width), BF16),
            ),
            in_specs=[vmem] * 2,
            out_specs=(vmem, vmem),
        )(next_latent, attention)
        return (next_latent, attention[None])

    return jax.shard_map(
        on_device,
        mesh=mesh,
        in_specs=(
            P("cfg", ("uly", "blk"), None),
            P("cfg", None, None),
            P(),
            P(("uly", "blk"), None),
            P(),
            P(),
            P(),
            P(),
            P("cfg", None, None),
            P(None, None, "uly"),
            P(),
        ),
        out_specs=(P(("uly", "blk"), None), P("cfg", ("uly", "blk"), None)),
        check_vma=False,
    )
```

```python
import functools
import math

import jax
import jax.numpy as jnp
import numpy as np
from jax import lax
from jax.experimental import pallas as pl
from jax.experimental.pallas import tpu as pltpu
from jax.sharding import PartitionSpec as P

HEAD_DIM = 128
GRID_H = 32
GRID_W = 32
CHAN = 64
EPS = 1e-6
MESH = pl.DeviceIdType.MESH
F32 = jnp.float32
BF16 = jnp.bfloat16


def pair_angles():
    time_dim = HEAD_DIM // 8
    space_dim = (HEAD_DIM - time_dim) // 2
    out = []
    for coords, width in ((8, time_dim), (GRID_H, space_dim), (GRID_W, space_dim)):
        freqs = 1.0 / 256.0 ** (np.arange(0, width, 2) / width)
        out.append(np.arange(coords)[:, None] * freqs[None, :])
    return out


def rope_tables(n_uly, n_y, n_z):
    time, row, col = pair_angles()
    n_x = n_uly // 2
    key = np.zeros((n_z, 2, 64, 2, n_y, GRID_W))
    query = np.zeros((n_y * n_z, 64, 2, 2, GRID_W))
    for half in range(2):
        for y in range(n_y):
            for z in range(n_z):
                at = row[2 * (y * n_z + z) + half]
                key[z, half, 8:36, :, y] = at[:, None, None]
                key[z, half, 36:64, :, y] = col.T[:, None]
                query[y * n_z + z, 8:36, :, half] = at[:, None, None]
                query[y * n_z + z, 36:64, :, half] = col.T[:, None]
    key = key.reshape(n_z, 2, 64, 128)
    query = query.reshape(n_y * n_z, 64, 128)
    frame = [2 * x + core for core in range(2) for x in range(n_x)]
    key_time = np.repeat(time[frame].T, n_y * GRID_W, axis=1)
    query_time = np.repeat(time.T, 2 * GRID_W, axis=1)

    def both(angles, axis):
        return np.stack([np.cos(angles), np.sin(angles)], axis=axis).astype(np.float32)

    return both(key, 2), both(key_time, 0), both(query, 1), both(query_time, 0)


def mm(a, b):
    return jnp.dot(a, b, preferred_element_type=F32)


def mm_nt(a, b, precision=None):
    return lax.dot_general(a, b, (((1,), (1,)), ((), ())), precision=precision, preferred_element_type=F32)


def split_bf16(value):
    high = value.astype(BF16)
    return high, (value - high.astype(F32)).astype(BF16)


def kernel(
    n_uly,
    n_y,
    n_z,
    guid_s,
    size_s,
    index_s,
    hidden_h,
    fmod_h,
    fw_h,
    latent_h,
    embed_h,
    bmod_h,
    w_h,
    gains_v,
    ktab_h,
    ktime_h,
    qtab_h,
    qtime_h,
    next_ref,
    out_ref,
    hidden_v,
    fmod_v,
    fw_v,
    latent_v,
    embed_v,
    bmod_v,
    w_v,
    ktab_v,
    ktime_v,
    qtab_v,
    qtime_v,
    vel_mine,
    vel_other,
    xp_v,
    lhs_v,
    gram_v,
    tk_v,
    tq_v,
    sv_v,
    aug_v,
    kt_v,
    q_v,
    acc_v,
    stage_v,
    load_sem,
    vel_send,
    vel_recv,
    plane_send,
    plane_recv,
    z_send,
    z_recv,
    group_send,
    group_recv,
    sib_send,
    sib_recv,
    out_send,
    out_recv,
    own_sem,
):
    cfg = lax.axis_index("cfg")
    uly = lax.axis_index("uly")
    blk = lax.axis_index("blk")
    x_at = uly // 2
    core = uly % 2
    sib = uly + 1 - 2 * core
    y_at = blk // n_z
    z_at = blk % n_z
    n_x = n_uly // 2
    half_rows = n_x * n_y * 32

    def remote(src, dst, send, recv, device):
        return pltpu.make_async_remote_copy(
            src_ref=src, dst_ref=dst, send_sem=send, recv_sem=recv, device_id=device, device_id_type=MESH
        )

    def near(dx, dy, dc):
        return (cfg, (x_at + dx) % n_x * 2 + (core + dc) % 2, (y_at + dy) % n_y * n_z + z_at)

    def ahead(off):
        return (cfg, uly, y_at * n_z + (z_at + n_z + off) % n_z)

    plane = [(dx, dy, dc) for dx in (2, 1, 3, 0) for dy in (1, 0) for dc in (1, 0) if dx + dy + dc > 0]
    side = [(dx, dy, 0) for dx in (2, 1, 3, 0) for dy in (1, 0) if dx + dy > 0]
    groups = [(1, 2), (3, n_z - 1)]
    leave = (2, 1, 3, 0)

    pairs = [
        (hidden_h, hidden_v),
        (fmod_h, fmod_v),
        (fw_h, fw_v),
        (latent_h, latent_v),
        (embed_h, embed_v),
        (bmod_h, bmod_v),
        (w_h.at[0], w_v.at[0]),
        (w_h.at[1], w_v.at[1]),
        (w_h.at[2], w_v.at[2]),
        (ktab_h, ktab_v),
        (ktime_h, ktime_v),
        (qtab_h.at[blk], qtab_v),
        (qtime_h, qtime_v),
    ]
    loads = [pltpu.make_async_copy(s, d, load_sem.at[i]) for i, (s, d) in enumerate(pairs)]
    for load in loads[:4]:
        load.start()

    barrier = pltpu.get_barrier_semaphore()
    for off in range(1, n_z):
        pl.semaphore_signal(barrier, inc=1, device_id=ahead(off), device_id_type=MESH)
    for offs in plane:
        pl.semaphore_signal(barrier, inc=1, device_id=near(*offs), device_id_type=MESH)
    pl.semaphore_signal(barrier, inc=1, device_id=(1 - cfg, uly, blk), device_id_type=MESH)

    for i in range(3):
        loads[i].wait()
    for load in loads[4:]:
        load.start()
    rows = hidden_v[...].astype(F32)
    mean = jnp.mean(rows, axis=1, keepdims=True)
    rows = rows - mean
    var = jnp.mean(rows * rows, axis=1, keepdims=True)
    rows = rows * lax.rsqrt(var + EPS)
    rows = (rows * (1.0 + fmod_v[1:2, :]) + fmod_v[0:1, :]).astype(BF16)
    vel = mm_nt(rows, fw_v[...])
    vel_mine[...] = jnp.concatenate([vel[0:32], vel[32:64]], axis=1)

    lanes = lax.broadcasted_iota(jnp.int32, (128, 128), 1)
    sublanes = lax.broadcasted_iota(jnp.int32, (128, 128), 0)
    source = jnp.where(sublanes < 64, 2 * sublanes, 2 * sublanes - 127)
    perm = jnp.where(lanes == source, 1.0, 0.0)
    perm_b = perm.astype(BF16)

    def prepare():
        loads[3].wait()
        loads[4].wait()
        loads[5].wait()
        emb = embed_v[...]
        emb = emb - jnp.mean(emb, axis=1, keepdims=True)
        high, low = split_bf16(emb)
        stack = jnp.concatenate([high, low], axis=0)
        gram = mm_nt(stack, stack)
        gram_v[...] = (gram[0:64, 0:64] + gram[0:64, 64:128] + gram[64:128, 0:64] + gram[64:128, 64:128]) * (1.0 / emb.shape[1])
        high, low = split_bf16(emb * (1.0 + bmod_v[1:2, :]))
        lhs_v[0:64, :] = high
        lhs_v[64:128, :] = low
        high, low = split_bf16(bmod_v[0:1, :])
        lhs_v[128:144, :] = jnp.concatenate([high, low, jnp.zeros((14, high.shape[1]), BF16)], axis=0)

    def project():
        lhs = lhs_v[...]
        for j in range(3):
            loads[6 + j].wait()
            full = mm(lhs, w_v[j])
            weight = full[0:64] + full[64:128]
            bias = full[128:129] + full[129:130]
            square = jnp.concatenate([weight, bias, jnp.zeros((63, weight.shape[1]), F32)], axis=0)
            high, low = split_bf16(square)
            for h in range(3):
                cols = slice(h * 128, h * 128 + 128)
                if j == 2:
                    sv_v[h, 0:128, :] = high[:, cols]
                    sv_v[h, 128:256, :] = low[:, cols]
                else:
                    target = tq_v if j == 0 else tk_v
                    target[cols, 0:128] = mm_nt(perm_b, high[:, cols]).astype(BF16)
                    target[cols, 128:256] = mm_nt(perm_b, low[:, cols]).astype(BF16)

    early = z_at < 3

    @pl.when(early)
    def _():
        prepare()
        project()

    pl.semaphore_wait(barrier, len(plane) + n_z)
    vel_copy = remote(vel_mine, vel_other, vel_send, vel_recv, (1 - cfg, uly, blk))
    vel_copy.start()
    pl.when(jnp.logical_not(early))(prepare)

    step = index_s[0]
    scale_now = guid_s[step]
    step_now = size_s[step]
    vel_copy.wait()
    mine = vel_mine[...]
    other = vel_other[...]
    cond = jnp.where(cfg == 0, mine, other)
    uncond = jnp.where(cfg == 0, other, mine)
    guided = uncond + scale_now * (cond - uncond)
    guided = jnp.concatenate([guided[:, 0:64], guided[:, 64:128]], axis=0)
    latent = latent_v[...] - step_now * guided
    next_ref[...] = latent
    power = jnp.dot(latent, gram_v[...], precision=lax.Precision.HIGHEST, preferred_element_type=F32)
    var = jnp.maximum(jnp.sum(power * latent, axis=1, keepdims=True), 0.0)
    normed = (latent * lax.rsqrt(var + EPS)).astype(BF16)
    own_at = ((core * n_x + x_at) * n_y + y_at) * 32
    own_rows = pl.ds(pl.multiple_of(own_at, 32), 32)
    own_half = pl.ds(pl.multiple_of(core * half_rows, half_rows), half_rows)
    sib_half = pl.ds(pl.multiple_of((1 - core) * half_rows, half_rows), half_rows)
    xp_v[0, own_rows, :] = jnp.concatenate([normed[0:32], normed[32:64]], axis=1)

    def rows_of(dx, dy, dc):
        at = ((core + dc) % 2 * n_x + (x_at + n_x - dx) % n_x) * n_y + (y_at + dy) % n_y
        return pl.ds(pl.multiple_of(at * 32, 32), 32)

    def offset(r):
        return (r + 1) // 2 * (2 * (r % 2) - 1)

    def z_copy(r):
        src = xp_v.at[0, own_rows, :]
        dst = xp_v.at[r, own_rows, :]
        return remote(src, dst, z_send.at[r - 1], z_recv.at[r - 1], ahead(-offset(r)))

    def plane_copy(k):
        there = xp_v.at[0, own_rows, :]
        return remote(there, there, plane_send.at[k], plane_recv.at[k], near(*plane[k]))

    def plane_from(k):
        there = xp_v.at[0, rows_of(*plane[k]), :]
        return remote(there, there, plane_send.at[k], plane_recv.at[k], near(*plane[k]))

    def group_copy(g, k):
        first, last = groups[g]
        there = xp_v.at[first : last + 1, own_rows, :]
        return remote(there, there, group_send.at[g, k], group_recv.at[g, k], near(*side[k]))

    def group_from(g, k):
        first, last = groups[g]
        there = xp_v.at[first : last + 1, rows_of(*side[k]), :]
        return remote(there, there, group_send.at[g, k], group_recv.at[g, k], near(*side[k]))

    def sib_copy(g):
        first, last = groups[g]
        there = xp_v.at[first : last + 1, own_half, :]
        return remote(there, there, sib_send.at[g], sib_recv.at[g], (cfg, sib, blk))

    def sib_from(g):
        first, last = groups[g]
        there = xp_v.at[first : last + 1, sib_half, :]
        return remote(there, there, sib_send.at[g], sib_recv.at[g], (cfg, sib, blk))

    def spread(g):
        first, last = groups[g]
        for r in range(first, last + 1):
            z_copy(r).wait_recv()
        for k in range(len(side)):
            group_copy(g, k).start()

    def share(g):
        for k in range(len(side)):
            group_from(g, k).wait_recv()
        sib_copy(g).start()

    for r in range(1, 3):
        z_copy(r).start()
    for k in range(len(plane)):
        plane_copy(k).start()
    for r in range(3, n_z):
        z_copy(r).start()

    pl.when(jnp.logical_not(early))(project)

    for i in range(9, 13):
        loads[i].wait()
    gains = jnp.concatenate([gains_v[...], jnp.zeros((6, 128), F32)], axis=0)
    gains = mm_nt(perm, gains, precision=lax.Precision.HIGHEST)
    ga_q = gains[0:64, 0:1] * (math.log2(math.e) / math.sqrt(HEAD_DIM))
    gb_q = gains[64:128, 0:1] * (math.log2(math.e) / math.sqrt(HEAD_DIM))
    ga_k = gains[0:64, 1:2]
    gb_k = gains[64:128, 1:2]

    one_hot = jnp.where(lax.broadcasted_iota(jnp.int32, (1, 128), 1) == 64, 1.0, 0.0)
    low_lanes = lax.broadcasted_iota(jnp.int32, (1, 128), 1) < 64

    def unpack(value):
        wide = value.astype(F32)
        first = jnp.where(low_lanes, wide, one_hot).astype(BF16)
        second = jnp.where(low_lanes, pltpu.roll(wide, 64, 1), one_hot).astype(BF16)
        return first, second

    def rope_tabs(ga, gb, cosine, sine):
        return ga * cosine, gb * sine, ga * sine, gb * cosine

    def rotate(proj, t1, t2, t3, t4):
        a, b = proj[0:64], proj[64:128]
        power = jnp.sum(a * a + b * b, axis=0, keepdims=True) * (1.0 / HEAD_DIM)
        scale = lax.rsqrt(power + EPS)
        return (a * t1 - b * t2) * scale, (a * t3 + b * t4) * scale

    def laid(time, rest, times):
        return jnp.concatenate([time, jnp.concatenate([rest] * times, axis=1)], axis=0)

    def make_keys(r):
        halves = unpack(xp_v[r])
        at = (z_at + n_z + offset(r)) % n_z
        size = 2 * half_rows
        times = rope_tabs(ga_k[0:8], gb_k[0:8], ktime_v[0], ktime_v[1])
        for half in range(2):
            cols = slice(half * size, half * size + size)
            aug_v[r, cols, :] = halves[half]
            proj = mm_nt(tk_v[...], jnp.concatenate([halves[half]] * 2, axis=1))
            rests = rope_tabs(ga_k[8:64], gb_k[8:64], ktab_v[at, half, 0, 8:64], ktab_v[at, half, 1, 8:64])
            tabs = [laid(t, r, size // 128) for t, r in zip(times, rests)]
            for h in range(3):
                ka, kb = rotate(proj[h * 128 : h * 128 + 128], *tabs)
                kt_v[r, h, 0:64, cols] = ka.astype(BF16)
                kt_v[r, h, 64:128, cols] = kb.astype(BF16)

    def attend(h, r, rows=slice(None)):
        scores = mm(q_v[h, rows], kt_v[r, h])
        return mm(jnp.exp2(scores).astype(BF16), aug_v[r])

    spread(0)
    for k in range(len(plane)):
        plane_from(k).wait_recv()

    parts = []
    for dx in leave:
        for c in range(2):
            at = (c * n_x + (x_at + dx) % n_x) * n_y + y_at
            parts += list(unpack(xp_v[0, pl.ds(pl.multiple_of(at * 32, 32), 32), :]))
    rows_q = jnp.concatenate(parts, axis=0)
    proj = mm_nt(tq_v[...], jnp.concatenate([rows_q, rows_q], axis=1))
    here = [pl.ds(pl.multiple_of((x_at + dx) % n_x * 128, 128), 128) for dx in leave]
    cos_t, sin_t = [jnp.concatenate([qtime_v[i, :, lanes] for lanes in here], axis=1) for i in range(2)]
    times = rope_tabs(ga_q[0:8], gb_q[0:8], cos_t, sin_t)
    rests = rope_tabs(ga_q[8:64], gb_q[8:64], qtab_v[0, 8:64], qtab_v[1, 8:64])
    tabs = [laid(t, r, n_uly * 64 // 128) for t, r in zip(times, rests)]
    for h in range(3):
        qa, qb = rotate(proj[h * 128 : h * 128 + 128], *tabs)
        q_v[h] = jnp.transpose(jnp.concatenate([qa, qb], axis=0)).astype(BF16)

    make_keys(0)
    acc_v[0] = attend(0, 0)
    spread(1)
    acc_v[1] = attend(1, 0)
    share(0)
    acc_v[2] = attend(2, 0)
    sib_from(0).wait_recv()

    make_keys(1)
    for h in range(2):
        acc_v[h] += attend(h, 1)
    make_keys(2)
    acc_v[2] += attend(2, 1)
    acc_v[0] += attend(0, 2)
    share(1)
    for h in range(1, 3):
        acc_v[h] += attend(h, 2)
    sib_from(1).wait_recv()
    make_keys(3)
    for h in range(3):
        acc_v[h] += attend(h, 3)
    for r in range(4, n_z):
        make_keys(r)

    width = 3 * HEAD_DIM

    def out_copy(j, dc, h=None):
        c = (core + dc) % 2
        rows = pl.ds(pl.multiple_of(j * 128 + c * 64, 64), 64)
        first, size = (0, width) if h is None else (h * 128, 128)
        src = stage_v.at[rows, first : first + size]
        dst = out_ref.at[:, pl.ds(pl.multiple_of(uly * width + first, 128), size)]
        if leave[j] + dc == 0:
            return pltpu.make_async_copy(src, dst, own_sem)
        to = (x_at + leave[j]) % n_x * 2 + c
        sem = (h or 0, j, dc)
        return remote(src, dst, out_send.at[sem], out_recv.at[sem], (cfg, to, blk))

    def out_from(j, dc, h=None):
        source = (x_at + n_x - leave[j]) % n_x * 2 + (core + dc) % 2
        first, size = (0, width) if h is None else (h * 128, 128)
        src = stage_v.at[0:64, first : first + size]
        dst = out_ref.at[:, pl.ds(pl.multiple_of(source * width + first, 128), size)]
        sem = (h or 0, j, dc)
        return remote(src, dst, out_send.at[sem], out_recv.at[sem], (cfg, source, blk))

    sends = [(0, 0, None), (0, 1, None), (1, 0, None), (1, 1, None)]
    sends += [(2, dc, h) for h in range(3) for dc in range(2)] + [(3, 1, None)]
    def finish(rows, h):
        numer = acc_v[h, rows]
        for r in range(4, n_z):
            numer += attend(h, r, rows)
        mean_x = numer * (1.0 / numer[:, 64:65])
        high, low = split_bf16(mean_x)
        result = mm(jnp.concatenate([high, high], axis=1), sv_v[h]) + mm(low, sv_v[h, 0:128])
        stage_v[rows, h * 128 : h * 128 + 128] = result.astype(BF16)

    for h in range(3):
        finish(slice(0, 256), h)
    for j in range(2):
        for dc in (1, 0):
            out_copy(j, dc).start()
    for h in range(2):
        finish(slice(256, 512), h)
        for dc in (1, 0):
            out_copy(2, dc, h).start()
    finish(slice(256, 384), 2)
    for dc in (1, 0):
        out_copy(2, dc, 2).start()
    finish(slice(384, 512), 2)
    for dc in (1, 0):
        out_copy(3, dc).start()

    for k in range(len(plane)):
        plane_copy(k).wait_send()
    for r in range(1, n_z):
        z_copy(r).wait_send()
    for g in range(len(groups)):
        for k in range(len(side)):
            group_copy(g, k).wait_send()
        sib_copy(g).wait_send()
    out_copy(3, 0).wait()
    for j, dc, h in sends:
        out_copy(j, dc, h).wait_send()
        out_from(j, dc, h).wait_recv()


def hand_over(next_in, out_in, next_ref, out_ref):
    next_ref[...] = next_in[...]
    out_ref[...] = out_in[...]


def solution(mesh):
    n_uly = mesh.shape["uly"]
    n_blk = mesh.shape["blk"]
    n_y = 2
    n_z = n_blk // n_y
    tables = rope_tables(n_uly, n_y, n_z)

    def on_device(
        hidden, final_mod, final_weight, latent, guidance, step_size, step_index, embed_weight, block_mod, qkv_weight, qk_gains
    ):
        smem = pl.BlockSpec(memory_space=pltpu.SMEM)
        vmem = pl.BlockSpec(memory_space=pltpu.VMEM)
        anywhere = pl.BlockSpec(memory_space=pl.ANY)
        rows, width = hidden.shape[1:]
        cols = qkv_weight.shape[2]
        heads = cols // HEAD_DIM
        keys = 64 * n_uly * n_y
        queries = rows * n_uly
        dma = pltpu.SemaphoreType.DMA
        next_latent, attention = pl.pallas_call(
            functools.partial(kernel, n_uly, n_y, n_z),
            out_shape=(pltpu.VMEM((rows, CHAN), F32), pltpu.VMEM((rows, width), BF16)),
            in_specs=[smem] * 3 + [anywhere] * 7 + [vmem] + [anywhere] * 4,
            out_specs=(vmem, vmem),
            scratch_shapes=[
                pltpu.VMEM((rows, width), BF16),
                pltpu.VMEM((2, width), F32),
                pltpu.VMEM((CHAN, width), BF16),
                pltpu.VMEM((rows, CHAN), F32),
                pltpu.VMEM((CHAN, width), F32),
                pltpu.VMEM((2, width), F32),
                pltpu.VMEM((3, width, cols), BF16),
                pltpu.VMEM(tables[0].shape, F32),
                pltpu.VMEM(tables[1].shape, F32),
                pltpu.VMEM(tables[2].shape[1:], F32),
                pltpu.VMEM(tables[3].shape, F32),
                pltpu.VMEM((32, 128), F32),
                pltpu.VMEM((32, 128), F32),
                pltpu.VMEM((n_z, n_uly * n_y * 32, 128), BF16),
                pltpu.VMEM((144, width), BF16),
                pltpu.VMEM((CHAN, CHAN), F32),
                pltpu.VMEM((cols, 256), BF16),
                pltpu.VMEM((cols, 256), BF16),
                pltpu.VMEM((heads, 256, 128), BF16),
                pltpu.VMEM((n_z, keys, 128), BF16),
                pltpu.VMEM((n_z, heads, 128, keys), BF16),
                pltpu.VMEM((heads, queries, 128), BF16),
                pltpu.VMEM((heads, queries, 128), F32),
                pltpu.VMEM((queries, cols), BF16),
                dma((13,)),
                dma,
                dma,
                dma((n_uly * n_y - 1,)),
                dma((n_uly * n_y - 1,)),
                dma((n_z - 1,)),
                dma((n_z - 1,)),
                dma((2, n_uly // 2 * n_y - 1)),
                dma((2, n_uly // 2 * n_y - 1)),
                dma((2,)),
                dma((2,)),
                dma((heads, n_uly // 2, 2)),
                dma((heads, n_uly // 2, 2)),
                dma,
            ],
            compiler_params=pltpu.CompilerParams(
                collective_id=0, has_side_effects=True, vmem_limit_bytes=56 << 20
            ),
        )(
            guidance,
            step_size,
            step_index,
            hidden[0],
            final_mod[0],
            final_weight.T,
            latent,
            embed_weight,
            block_mod[0],
            jnp.transpose(qkv_weight, (1, 0, 2)),
            qk_gains,
            *[jnp.asarray(t) for t in tables],
        )
        next_latent, attention = pl.pallas_call(
            hand_over,
            out_shape=(
                jax.ShapeDtypeStruct((rows, CHAN), F32),
                jax.ShapeDtypeStruct((rows, width), BF16),
            ),
            in_specs=[vmem] * 2,
            out_specs=(vmem, vmem),
        )(next_latent, attention)
        return (next_latent, attention[None])

    return jax.shard_map(
        on_device,
        mesh=mesh,
        in_specs=(
            P("cfg", ("uly", "blk"), None),
            P("cfg", None, None),
            P(),
            P(("uly", "blk"), None),
            P(),
            P(),
            P(),
            P(),
            P("cfg", None, None),
            P(None, None, "uly"),
            P(),
        ),
        out_specs=(P(("uly", "blk"), None), P("cfg", ("uly", "blk"), None)),
        check_vma=False,
    )
```

```python
import functools
import math

import jax
import jax.numpy as jnp
import numpy as np
from jax import lax
from jax.experimental import pallas as pl
from jax.experimental.pallas import tpu as pltpu
from jax.sharding import PartitionSpec as P

HEAD_DIM = 128
GRID_H = 32
GRID_W = 32
CHAN = 64
EPS = 1e-6
MESH = pl.DeviceIdType.MESH
F32 = jnp.float32
BF16 = jnp.bfloat16


def pair_angles():
    time_dim = HEAD_DIM // 8
    space_dim = (HEAD_DIM - time_dim) // 2
    out = []
    for coords, width in ((8, time_dim), (GRID_H, space_dim), (GRID_W, space_dim)):
        freqs = 1.0 / 256.0 ** (np.arange(0, width, 2) / width)
        out.append(np.arange(coords)[:, None] * freqs[None, :])
    return out


def rope_tables(n_uly, n_y, n_z):
    time, row, col = pair_angles()
    n_x = n_uly // 2
    key = np.zeros((n_z, 2, 64, 2, n_y, GRID_W))
    query = np.zeros((n_y * n_z, 64, 2, 2, GRID_W))
    for half in range(2):
        for y in range(n_y):
            for z in range(n_z):
                at = row[2 * (y * n_z + z) + half]
                key[z, half, 8:36, :, y] = at[:, None, None]
                key[z, half, 36:64, :, y] = col.T[:, None]
                query[y * n_z + z, 8:36, :, half] = at[:, None, None]
                query[y * n_z + z, 36:64, :, half] = col.T[:, None]
    key = key.reshape(n_z, 2, 64, 128)
    query = query.reshape(n_y * n_z, 64, 128)
    frame = [2 * x + core for core in range(2) for x in range(n_x)]
    key_time = np.repeat(time[frame].T, n_y * GRID_W, axis=1)
    query_time = np.repeat(time.T, 2 * GRID_W, axis=1)

    def both(angles, axis):
        return np.stack([np.cos(angles), np.sin(angles)], axis=axis).astype(np.float32)

    return both(key, 2), both(key_time, 0), both(query, 1), both(query_time, 0)


def mm(a, b):
    return jnp.dot(a, b, preferred_element_type=F32)


def mm_nt(a, b, precision=None):
    return lax.dot_general(a, b, (((1,), (1,)), ((), ())), precision=precision, preferred_element_type=F32)


def split_bf16(value):
    high = value.astype(BF16)
    return high, (value - high.astype(F32)).astype(BF16)


def kernel(
    n_uly,
    n_y,
    n_z,
    guid_s,
    size_s,
    index_s,
    hidden_h,
    fmod_h,
    fw_h,
    latent_h,
    embed_h,
    bmod_h,
    w_h,
    gains_v,
    ktab_h,
    ktime_h,
    qtab_h,
    qtime_h,
    next_ref,
    out_ref,
    hidden_v,
    fmod_v,
    fw_v,
    latent_v,
    embed_v,
    bmod_v,
    w_v,
    ktab_v,
    ktime_v,
    qtab_v,
    qtime_v,
    vel_mine,
    vel_other,
    xp_v,
    lhs_v,
    gram_v,
    tk_v,
    tq_v,
    sv_v,
    aug_v,
    kt_v,
    q_v,
    acc_v,
    stage_v,
    load_sem,
    vel_send,
    vel_recv,
    plane_send,
    plane_recv,
    z_send,
    z_recv,
    group_send,
    group_recv,
    sib_send,
    sib_recv,
    out_send,
    out_recv,
    own_sem,
):
    cfg = lax.axis_index("cfg")
    uly = lax.axis_index("uly")
    blk = lax.axis_index("blk")
    x_at = uly // 2
    core = uly % 2
    sib = uly + 1 - 2 * core
    y_at = blk // n_z
    z_at = blk % n_z
    n_x = n_uly // 2
    half_rows = n_x * n_y * 32

    def remote(src, dst, send, recv, device):
        return pltpu.make_async_remote_copy(
            src_ref=src, dst_ref=dst, send_sem=send, recv_sem=recv, device_id=device, device_id_type=MESH
        )

    def near(dx, dy, dc):
        return (cfg, (x_at + dx) % n_x * 2 + (core + dc) % 2, (y_at + dy) % n_y * n_z + z_at)

    def ahead(off):
        return (cfg, uly, y_at * n_z + (z_at + n_z + off) % n_z)

    plane = [(dx, dy, dc) for dx in (2, 1, 3, 0) for dy in (1, 0) for dc in (1, 0) if dx + dy + dc > 0]
    side = [(dx, dy, 0) for dx in (2, 1, 3, 0) for dy in (1, 0) if dx + dy > 0]
    groups = [(1, 2), (3, n_z - 1)]
    leave = (2, 1, 3, 0)

    pairs = [
        (hidden_h, hidden_v),
        (fmod_h, fmod_v),
        (fw_h, fw_v),
        (latent_h, latent_v),
        (embed_h, embed_v),
        (bmod_h, bmod_v),
        (w_h.at[0], w_v.at[0]),
        (w_h.at[1], w_v.at[1]),
        (w_h.at[2], w_v.at[2]),
        (ktab_h, ktab_v),
        (ktime_h, ktime_v),
        (qtab_h.at[blk], qtab_v),
        (qtime_h, qtime_v),
    ]
    loads = [pltpu.make_async_copy(s, d, load_sem.at[i]) for i, (s, d) in enumerate(pairs)]
    for load in loads[:4]:
        load.start()

    barrier = pltpu.get_barrier_semaphore()
    for off in range(1, n_z):
        pl.semaphore_signal(barrier, inc=1, device_id=ahead(off), device_id_type=MESH)
    for offs in plane:
        pl.semaphore_signal(barrier, inc=1, device_id=near(*offs), device_id_type=MESH)
    pl.semaphore_signal(barrier, inc=1, device_id=(1 - cfg, uly, blk), device_id_type=MESH)

    for i in range(3):
        loads[i].wait()
    for load in loads[4:]:
        load.start()
    rows = hidden_v[...].astype(F32)
    mean = jnp.mean(rows, axis=1, keepdims=True)
    rows = rows - mean
    var = jnp.mean(rows * rows, axis=1, keepdims=True)
    rows = rows * lax.rsqrt(var + EPS)
    rows = (rows * (1.0 + fmod_v[1:2, :]) + fmod_v[0:1, :]).astype(BF16)
    vel = mm_nt(rows, fw_v[...])
    vel_mine[...] = jnp.concatenate([vel[0:32], vel[32:64]], axis=1)

    lanes = lax.broadcasted_iota(jnp.int32, (128, 128), 1)
    sublanes = lax.broadcasted_iota(jnp.int32, (128, 128), 0)
    source = jnp.where(sublanes < 64, 2 * sublanes, 2 * sublanes - 127)
    perm = jnp.where(lanes == source, 1.0, 0.0)
    perm_b = perm.astype(BF16)

    def prepare():
        loads[3].wait()
        loads[4].wait()
        loads[5].wait()
        emb = embed_v[...]
        emb = emb - jnp.mean(emb, axis=1, keepdims=True)
        high, low = split_bf16(emb)
        stack = jnp.concatenate([high, low], axis=0)
        gram = mm_nt(stack, stack)
        gram_v[...] = (gram[0:64, 0:64] + gram[0:64, 64:128] + gram[64:128, 0:64] + gram[64:128, 64:128]) * (1.0 / emb.shape[1])
        high, low = split_bf16(emb * (1.0 + bmod_v[1:2, :]))
        lhs_v[0:64, :] = high
        lhs_v[64:128, :] = low
        high, low = split_bf16(bmod_v[0:1, :])
        lhs_v[128:144, :] = jnp.concatenate([high, low, jnp.zeros((14, high.shape[1]), BF16)], axis=0)

    def project():
        lhs = lhs_v[...]
        for j in range(3):
            loads[6 + j].wait()
            full = mm(lhs, w_v[j])
            weight = full[0:64] + full[64:128]
            bias = full[128:129] + full[129:130]
            square = jnp.concatenate([weight, bias, jnp.zeros((63, weight.shape[1]), F32)], axis=0)
            high, low = split_bf16(square)
            for h in range(3):
                cols = slice(h * 128, h * 128 + 128)
                if j == 2:
                    sv_v[h, 0:128, :] = high[:, cols]
                    sv_v[h, 128:256, :] = low[:, cols]
                else:
                    target = tq_v if j == 0 else tk_v
                    target[cols, 0:128] = mm_nt(perm_b, high[:, cols]).astype(BF16)
                    target[cols, 128:256] = mm_nt(perm_b, low[:, cols]).astype(BF16)

    early = z_at < 3

    @pl.when(early)
    def _():
        prepare()
        project()

    pl.semaphore_wait(barrier, len(plane) + n_z)
    vel_copy = remote(vel_mine, vel_other, vel_send, vel_recv, (1 - cfg, uly, blk))
    vel_copy.start()
    pl.when(jnp.logical_not(early))(prepare)

    step = index_s[0]
    scale_now = guid_s[step]
    step_now = size_s[step]
    vel_copy.wait()
    mine = vel_mine[...]
    other = vel_other[...]
    cond = jnp.where(cfg == 0, mine, other)
    uncond = jnp.where(cfg == 0, other, mine)
    guided = uncond + scale_now * (cond - uncond)
    guided = jnp.concatenate([guided[:, 0:64], guided[:, 64:128]], axis=0)
    latent = latent_v[...] - step_now * guided
    next_ref[...] = latent
    power = jnp.dot(latent, gram_v[...], precision=lax.Precision.HIGHEST, preferred_element_type=F32)
    var = jnp.maximum(jnp.sum(power * latent, axis=1, keepdims=True), 0.0)
    normed = (latent * lax.rsqrt(var + EPS)).astype(BF16)
    own_at = ((core * n_x + x_at) * n_y + y_at) * 32
    own_rows = pl.ds(pl.multiple_of(own_at, 32), 32)
    own_half = pl.ds(pl.multiple_of(core * half_rows, half_rows), half_rows)
    sib_half = pl.ds(pl.multiple_of((1 - core) * half_rows, half_rows), half_rows)
    xp_v[0, own_rows, :] = jnp.concatenate([normed[0:32], normed[32:64]], axis=1)

    def rows_of(dx, dy, dc):
        at = ((core + dc) % 2 * n_x + (x_at + n_x - dx) % n_x) * n_y + (y_at + dy) % n_y
        return pl.ds(pl.multiple_of(at * 32, 32), 32)

    def offset(r):
        return (r + 1) // 2 * (2 * (r % 2) - 1)

    def z_copy(r):
        src = xp_v.at[0, own_rows, :]
        dst = xp_v.at[r, own_rows, :]
        return remote(src, dst, z_send.at[r - 1], z_recv.at[r - 1], ahead(-offset(r)))

    def plane_copy(k):
        there = xp_v.at[0, own_rows, :]
        return remote(there, there, plane_send.at[k], plane_recv.at[k], near(*plane[k]))

    def plane_from(k):
        there = xp_v.at[0, rows_of(*plane[k]), :]
        return remote(there, there, plane_send.at[k], plane_recv.at[k], near(*plane[k]))

    def group_copy(g, k):
        first, last = groups[g]
        there = xp_v.at[first : last + 1, own_rows, :]
        return remote(there, there, group_send.at[g, k], group_recv.at[g, k], near(*side[k]))

    def group_from(g, k):
        first, last = groups[g]
        there = xp_v.at[first : last + 1, rows_of(*side[k]), :]
        return remote(there, there, group_send.at[g, k], group_recv.at[g, k], near(*side[k]))

    def sib_copy(g):
        first, last = groups[g]
        there = xp_v.at[first : last + 1, own_half, :]
        return remote(there, there, sib_send.at[g], sib_recv.at[g], (cfg, sib, blk))

    def sib_from(g):
        first, last = groups[g]
        there = xp_v.at[first : last + 1, sib_half, :]
        return remote(there, there, sib_send.at[g], sib_recv.at[g], (cfg, sib, blk))

    def spread(g):
        first, last = groups[g]
        for r in range(first, last + 1):
            z_copy(r).wait_recv()
        for k in range(len(side)):
            group_copy(g, k).start()

    def share(g):
        for k in range(len(side)):
            group_from(g, k).wait_recv()
        sib_copy(g).start()

    for r in range(1, 3):
        z_copy(r).start()
    for k in range(len(plane)):
        plane_copy(k).start()
    for r in range(3, n_z):
        z_copy(r).start()

    pl.when(jnp.logical_not(early))(project)

    for i in range(9, 13):
        loads[i].wait()
    gains = jnp.concatenate([gains_v[...], jnp.zeros((6, 128), F32)], axis=0)
    gains = mm_nt(perm, gains, precision=lax.Precision.HIGHEST)
    ga_q = gains[0:64, 0:1] * (math.log2(math.e) / math.sqrt(HEAD_DIM))
    gb_q = gains[64:128, 0:1] * (math.log2(math.e) / math.sqrt(HEAD_DIM))
    ga_k = gains[0:64, 1:2]
    gb_k = gains[64:128, 1:2]

    one_hot = jnp.where(lax.broadcasted_iota(jnp.int32, (1, 128), 1) == 64, 1.0, 0.0)
    low_lanes = lax.broadcasted_iota(jnp.int32, (1, 128), 1) < 64

    def unpack(value):
        wide = value.astype(F32)
        first = jnp.where(low_lanes, wide, one_hot).astype(BF16)
        second = jnp.where(low_lanes, pltpu.roll(wide, 64, 1), one_hot).astype(BF16)
        return first, second

    def rope_tabs(ga, gb, cosine, sine):
        return ga * cosine, gb * sine, ga * sine, gb * cosine

    def rotate(proj, t1, t2, t3, t4):
        a, b = proj[0:64], proj[64:128]
        power = jnp.sum(a * a + b * b, axis=0, keepdims=True) * (1.0 / HEAD_DIM)
        scale = lax.rsqrt(power + EPS)
        return (a * t1 - b * t2) * scale, (a * t3 + b * t4) * scale

    def laid(time, rest, times):
        return jnp.concatenate([time, jnp.concatenate([rest] * times, axis=1)], axis=0)

    def make_keys(r):
        halves = unpack(xp_v[r])
        at = (z_at + n_z + offset(r)) % n_z
        size = 2 * half_rows
        times = rope_tabs(ga_k[0:8], gb_k[0:8], ktime_v[0], ktime_v[1])
        for half in range(2):
            cols = slice(half * size, half * size + size)
            aug_v[r, cols, :] = halves[half]
            proj = mm_nt(tk_v[...], jnp.concatenate([halves[half]] * 2, axis=1))
            rests = rope_tabs(ga_k[8:64], gb_k[8:64], ktab_v[at, half, 0, 8:64], ktab_v[at, half, 1, 8:64])
            tabs = [laid(t, r, size // 128) for t, r in zip(times, rests)]
            for h in range(3):
                ka, kb = rotate(proj[h * 128 : h * 128 + 128], *tabs)
                kt_v[r, h, 0:64, cols] = ka.astype(BF16)
                kt_v[r, h, 64:128, cols] = kb.astype(BF16)

    def attend(h, r, rows=slice(None)):
        scores = mm(q_v[h, rows], kt_v[r, h])
        return mm(jnp.exp2(scores).astype(BF16), aug_v[r])

    spread(0)
    for k in range(len(plane)):
        plane_from(k).wait_recv()

    parts = []
    for dx in leave:
        for c in range(2):
            at = (c * n_x + (x_at + dx) % n_x) * n_y + y_at
            parts += list(unpack(xp_v[0, pl.ds(pl.multiple_of(at * 32, 32), 32), :]))
    rows_q = jnp.concatenate(parts, axis=0)
    proj = mm_nt(tq_v[...], jnp.concatenate([rows_q, rows_q], axis=1))
    here = [pl.ds(pl.multiple_of((x_at + dx) % n_x * 128, 128), 128) for dx in leave]
    cos_t, sin_t = [jnp.concatenate([qtime_v[i, :, lanes] for lanes in here], axis=1) for i in range(2)]
    times = rope_tabs(ga_q[0:8], gb_q[0:8], cos_t, sin_t)
    rests = rope_tabs(ga_q[8:64], gb_q[8:64], qtab_v[0, 8:64], qtab_v[1, 8:64])
    tabs = [laid(t, r, n_uly * 64 // 128) for t, r in zip(times, rests)]
    for h in range(3):
        qa, qb = rotate(proj[h * 128 : h * 128 + 128], *tabs)
        q_v[h] = jnp.transpose(jnp.concatenate([qa, qb], axis=0)).astype(BF16)

    make_keys(0)
    acc_v[0] = attend(0, 0)
    spread(1)
    acc_v[1] = attend(1, 0)
    share(0)
    acc_v[2] = attend(2, 0)
    sib_from(0).wait_recv()

    make_keys(1)
    for h in range(2):
        acc_v[h] += attend(h, 1)
    make_keys(2)
    acc_v[2] += attend(2, 1)
    acc_v[0] += attend(0, 2)
    share(1)
    for h in range(1, 3):
        acc_v[h] += attend(h, 2)
    sib_from(1).wait_recv()
    make_keys(3)
    for h in range(3):
        acc_v[h] += attend(h, 3)
    for r in range(4, n_z):
        make_keys(r)

    width = 3 * HEAD_DIM

    def out_copy(j, dc, h=None):
        c = (core + dc) % 2
        rows = pl.ds(pl.multiple_of(j * 128 + c * 64, 64), 64)
        first, size = (0, width) if h is None else (h * 128, 128)
        src = stage_v.at[rows, first : first + size]
        dst = out_ref.at[:, pl.ds(pl.multiple_of(uly * width + first, 128), size)]
        if leave[j] + dc == 0:
            return pltpu.make_async_copy(src, dst, own_sem)
        to = (x_at + leave[j]) % n_x * 2 + c
        sem = (h or 0, j, dc)
        return remote(src, dst, out_send.at[sem], out_recv.at[sem], (cfg, to, blk))

    def out_from(j, dc, h=None):
        source = (x_at + n_x - leave[j]) % n_x * 2 + (core + dc) % 2
        first, size = (0, width) if h is None else (h * 128, 128)
        src = stage_v.at[0:64, first : first + size]
        dst = out_ref.at[:, pl.ds(pl.multiple_of(source * width + first, 128), size)]
        sem = (h or 0, j, dc)
        return remote(src, dst, out_send.at[sem], out_recv.at[sem], (cfg, source, blk))

    sends = [(0, 0, None), (0, 1, None), (1, 0, None), (1, 1, None)]
    sends += [(2, dc, h) for h in range(3) for dc in range(2)] + [(3, 1, None)]
    def finish(rows, h):
        numer = acc_v[h, rows]
        for r in range(4, n_z):
            numer += attend(h, r, rows)
        mean_x = numer * (1.0 / numer[:, 64:65])
        high, low = split_bf16(mean_x)
        result = mm(jnp.concatenate([high, high], axis=1), sv_v[h]) + mm(low, sv_v[h, 0:128])
        stage_v[rows, h * 128 : h * 128 + 128] = result.astype(BF16)

    for h in range(3):
        finish(slice(0, 256), h)
    for j in range(2):
        for dc in (1, 0):
            out_copy(j, dc).start()
    for h in range(2):
        finish(slice(256, 512), h)
        for dc in (1, 0):
            out_copy(2, dc, h).start()
    finish(slice(256, 384), 2)
    for dc in (1, 0):
        out_copy(2, dc, 2).start()
    finish(slice(384, 512), 2)
    for dc in (1, 0):
        out_copy(3, dc).start()

    for k in range(len(plane)):
        plane_copy(k).wait_send()
    for r in range(1, n_z):
        z_copy(r).wait_send()
    for g in range(len(groups)):
        for k in range(len(side)):
            group_copy(g, k).wait_send()
        sib_copy(g).wait_send()
    out_copy(3, 0).wait()
    for j, dc, h in sends:
        out_copy(j, dc, h).wait_send()
        out_from(j, dc, h).wait_recv()


def hand_over(next_in, out_in, next_ref, out_ref, sems):
    copies = [
        pltpu.make_async_copy(out_in, out_ref, sems.at[0]),
        pltpu.make_async_copy(next_in, next_ref, sems.at[1]),
    ]
    for copy in copies:
        copy.start()
    for copy in copies:
        copy.wait()


def solution(mesh):
    n_uly = mesh.shape["uly"]
    n_blk = mesh.shape["blk"]
    n_y = 2
    n_z = n_blk // n_y
    tables = rope_tables(n_uly, n_y, n_z)

    def on_device(
        hidden, final_mod, final_weight, latent, guidance, step_size, step_index, embed_weight, block_mod, qkv_weight, qk_gains
    ):
        smem = pl.BlockSpec(memory_space=pltpu.SMEM)
        vmem = pl.BlockSpec(memory_space=pltpu.VMEM)
        anywhere = pl.BlockSpec(memory_space=pl.ANY)
        rows, width = hidden.shape[1:]
        cols = qkv_weight.shape[2]
        heads = cols // HEAD_DIM
        keys = 64 * n_uly * n_y
        queries = rows * n_uly
        dma = pltpu.SemaphoreType.DMA
        next_latent, attention = pl.pallas_call(
            functools.partial(kernel, n_uly, n_y, n_z),
            out_shape=(pltpu.VMEM((rows, CHAN), F32), pltpu.VMEM((rows, width), BF16)),
            in_specs=[smem] * 3 + [anywhere] * 7 + [vmem] + [anywhere] * 4,
            out_specs=(vmem, vmem),
            scratch_shapes=[
                pltpu.VMEM((rows, width), BF16),
                pltpu.VMEM((2, width), F32),
                pltpu.VMEM((CHAN, width), BF16),
                pltpu.VMEM((rows, CHAN), F32),
                pltpu.VMEM((CHAN, width), F32),
                pltpu.VMEM((2, width), F32),
                pltpu.VMEM((3, width, cols), BF16),
                pltpu.VMEM(tables[0].shape, F32),
                pltpu.VMEM(tables[1].shape, F32),
                pltpu.VMEM(tables[2].shape[1:], F32),
                pltpu.VMEM(tables[3].shape, F32),
                pltpu.VMEM((32, 128), F32),
                pltpu.VMEM((32, 128), F32),
                pltpu.VMEM((n_z, n_uly * n_y * 32, 128), BF16),
                pltpu.VMEM((144, width), BF16),
                pltpu.VMEM((CHAN, CHAN), F32),
                pltpu.VMEM((cols, 256), BF16),
                pltpu.VMEM((cols, 256), BF16),
                pltpu.VMEM((heads, 256, 128), BF16),
                pltpu.VMEM((n_z, keys, 128), BF16),
                pltpu.VMEM((n_z, heads, 128, keys), BF16),
                pltpu.VMEM((heads, queries, 128), BF16),
                pltpu.VMEM((heads, queries, 128), F32),
                pltpu.VMEM((queries, cols), BF16),
                dma((13,)),
                dma,
                dma,
                dma((n_uly * n_y - 1,)),
                dma((n_uly * n_y - 1,)),
                dma((n_z - 1,)),
                dma((n_z - 1,)),
                dma((2, n_uly // 2 * n_y - 1)),
                dma((2, n_uly // 2 * n_y - 1)),
                dma((2,)),
                dma((2,)),
                dma((heads, n_uly // 2, 2)),
                dma((heads, n_uly // 2, 2)),
                dma,
            ],
            compiler_params=pltpu.CompilerParams(
                collective_id=0, has_side_effects=True, vmem_limit_bytes=56 << 20
            ),
        )(
            guidance,
            step_size,
            step_index,
            hidden[0],
            final_mod[0],
            final_weight.T,
            latent,
            embed_weight,
            block_mod[0],
            jnp.transpose(qkv_weight, (1, 0, 2)),
            qk_gains,
            *[jnp.asarray(t) for t in tables],
        )
        next_latent, attention = pl.pallas_call(
            hand_over,
            out_shape=(
                jax.ShapeDtypeStruct((rows, CHAN), F32),
                jax.ShapeDtypeStruct((rows, width), BF16),
            ),
            in_specs=[vmem] * 2,
            out_specs=(anywhere, anywhere),
            scratch_shapes=[dma((2,))],
        )(
            pltpu.with_memory_space_constraint(next_latent, pltpu.VMEM),
            pltpu.with_memory_space_constraint(attention, pltpu.VMEM),
        )
        return (next_latent, attention[None])

    return jax.shard_map(
        on_device,
        mesh=mesh,
        in_specs=(
            P("cfg", ("uly", "blk"), None),
            P("cfg", None, None),
            P(),
            P(("uly", "blk"), None),
            P(),
            P(),
            P(),
            P(),
            P("cfg", None, None),
            P(None, None, "uly"),
            P(),
        ),
        out_specs=(P(("uly", "blk"), None), P("cfg", ("uly", "blk"), None)),
        check_vma=False,
    )
```

```python
import functools
import math

import jax
import jax.numpy as jnp
import numpy as np
from jax import lax
from jax.experimental import pallas as pl
from jax.experimental.pallas import tpu as pltpu
from jax.sharding import PartitionSpec as P

HEAD_DIM = 128
GRID_H = 32
GRID_W = 32
CHAN = 64
EPS = 1e-6
MESH = pl.DeviceIdType.MESH
F32 = jnp.float32
BF16 = jnp.bfloat16


def pair_angles():
    time_dim = HEAD_DIM // 8
    space_dim = (HEAD_DIM - time_dim) // 2
    out = []
    for coords, width in ((8, time_dim), (GRID_H, space_dim), (GRID_W, space_dim)):
        freqs = 1.0 / 256.0 ** (np.arange(0, width, 2) / width)
        out.append(np.arange(coords)[:, None] * freqs[None, :])
    return out


def rope_tables(n_uly, n_y, n_z):
    time, row, col = pair_angles()
    n_x = n_uly // 2
    key = np.zeros((n_z, 2, 64, 2, n_y, GRID_W))
    query = np.zeros((n_y * n_z, 64, 2, 2, GRID_W))
    for half in range(2):
        for y in range(n_y):
            for z in range(n_z):
                at = row[2 * (y * n_z + z) + half]
                key[z, half, 8:36, :, y] = at[:, None, None]
                key[z, half, 36:64, :, y] = col.T[:, None]
                query[y * n_z + z, 8:36, :, half] = at[:, None, None]
                query[y * n_z + z, 36:64, :, half] = col.T[:, None]
    key = key.reshape(n_z, 2, 64, 128)
    query = query.reshape(n_y * n_z, 64, 128)
    frame = [2 * x + core for core in range(2) for x in range(n_x)]
    key_time = np.repeat(time[frame].T, n_y * GRID_W, axis=1)
    query_time = np.repeat(time.T, 2 * GRID_W, axis=1)

    def both(angles, axis):
        return np.stack([np.cos(angles), np.sin(angles)], axis=axis).astype(np.float32)

    return both(key, 2), both(key_time, 0), both(query, 1), both(query_time, 0)


def mm(a, b):
    return jnp.dot(a, b, preferred_element_type=F32)


def mm_nt(a, b, precision=None):
    return lax.dot_general(a, b, (((1,), (1,)), ((), ())), precision=precision, preferred_element_type=F32)


def split_bf16(value):
    high = value.astype(BF16)
    return high, (value - high.astype(F32)).astype(BF16)


def kernel(
    n_uly,
    n_y,
    n_z,
    guid_s,
    size_s,
    index_s,
    hidden_h,
    fmod_h,
    fw_h,
    latent_h,
    embed_h,
    bmod_h,
    w_h,
    gains_v,
    ktab_h,
    ktime_h,
    qtab_h,
    qtime_h,
    next_ref,
    out_ref,
    hidden_v,
    fmod_v,
    fw_v,
    latent_v,
    embed_v,
    bmod_v,
    w_v,
    ktab_v,
    ktime_v,
    qtab_v,
    qtime_v,
    vel_mine,
    vel_other,
    xp_v,
    lhs_v,
    gram_v,
    tk_v,
    tq_v,
    sv_v,
    aug_v,
    kt_v,
    q_v,
    acc_v,
    stage_v,
    load_sem,
    vel_send,
    vel_recv,
    plane_send,
    plane_recv,
    z_send,
    z_recv,
    group_send,
    group_recv,
    sib_send,
    sib_recv,
    out_send,
    out_recv,
    own_sem,
    relay,
):
    cfg = lax.axis_index("cfg")
    uly = lax.axis_index("uly")
    blk = lax.axis_index("blk")
    x_at = uly // 2
    core = uly % 2
    sib = uly + 1 - 2 * core
    y_at = blk // n_z
    z_at = blk % n_z
    n_x = n_uly // 2
    half_rows = n_x * n_y * 32

    def remote(src, dst, send, recv, device):
        return pltpu.make_async_remote_copy(
            src_ref=src, dst_ref=dst, send_sem=send, recv_sem=recv, device_id=device, device_id_type=MESH
        )

    def near(dx, dy, dc):
        return (cfg, (x_at + dx) % n_x * 2 + (core + dc) % 2, (y_at + dy) % n_y * n_z + z_at)

    def ahead(off):
        return (cfg, uly, y_at * n_z + (z_at + n_z + off) % n_z)

    plane = [(dx, dy, dc) for dx in (2, 1, 3, 0) for dy in (1, 0) for dc in (1, 0) if dx + dy + dc > 0]
    side = [(dx, dy, 0) for dx in (2, 1, 3, 0) for dy in (1, 0) if dx + dy > 0]
    groups = [(1, 2), (3, n_z - 1)]
    leave = (2, 1, 3, 0)

    pairs = [
        (hidden_h, hidden_v),
        (fmod_h, fmod_v),
        (fw_h, fw_v),
        (latent_h, latent_v),
        (embed_h, embed_v),
        (bmod_h, bmod_v),
        (w_h.at[0], w_v.at[0]),
        (w_h.at[1], w_v.at[1]),
        (w_h.at[2], w_v.at[2]),
        (ktab_h, ktab_v),
        (ktime_h, ktime_v),
        (qtab_h.at[blk], qtab_v),
        (qtime_h, qtime_v),
    ]
    loads = [pltpu.make_async_copy(s, d, load_sem.at[i]) for i, (s, d) in enumerate(pairs)]
    for load in loads[:4]:
        load.start()

    barrier = pltpu.get_barrier_semaphore()
    for off in (1, -1):
        pl.semaphore_signal(barrier, inc=1, device_id=ahead(off), device_id_type=MESH)
    for offs in plane:
        pl.semaphore_signal(barrier, inc=1, device_id=near(*offs), device_id_type=MESH)
    pl.semaphore_signal(barrier, inc=1, device_id=(1 - cfg, uly, blk), device_id_type=MESH)

    for i in range(3):
        loads[i].wait()
    for load in loads[4:]:
        load.start()
    rows = hidden_v[...].astype(F32)
    mean = jnp.mean(rows, axis=1, keepdims=True)
    rows = rows - mean
    var = jnp.mean(rows * rows, axis=1, keepdims=True)
    rows = rows * lax.rsqrt(var + EPS)
    rows = (rows * (1.0 + fmod_v[1:2, :]) + fmod_v[0:1, :]).astype(BF16)
    vel = mm_nt(rows, fw_v[...])
    vel_mine[...] = jnp.concatenate([vel[0:32], vel[32:64]], axis=1)

    lanes = lax.broadcasted_iota(jnp.int32, (128, 128), 1)
    sublanes = lax.broadcasted_iota(jnp.int32, (128, 128), 0)
    source = jnp.where(sublanes < 64, 2 * sublanes, 2 * sublanes - 127)
    perm = jnp.where(lanes == source, 1.0, 0.0)
    perm_b = perm.astype(BF16)

    def prepare():
        loads[3].wait()
        loads[4].wait()
        loads[5].wait()
        emb = embed_v[...]
        emb = emb - jnp.mean(emb, axis=1, keepdims=True)
        high, low = split_bf16(emb)
        stack = jnp.concatenate([high, low], axis=0)
        gram = mm_nt(stack, stack)
        gram_v[...] = (gram[0:64, 0:64] + gram[0:64, 64:128] + gram[64:128, 0:64] + gram[64:128, 64:128]) * (1.0 / emb.shape[1])
        high, low = split_bf16(emb * (1.0 + bmod_v[1:2, :]))
        lhs_v[0:64, :] = high
        lhs_v[64:128, :] = low
        high, low = split_bf16(bmod_v[0:1, :])
        lhs_v[128:144, :] = jnp.concatenate([high, low, jnp.zeros((14, high.shape[1]), BF16)], axis=0)

    def project():
        lhs = lhs_v[...]
        for j in range(3):
            loads[6 + j].wait()
            full = mm(lhs, w_v[j])
            weight = full[0:64] + full[64:128]
            bias = full[128:129] + full[129:130]
            square = jnp.concatenate([weight, bias, jnp.zeros((63, weight.shape[1]), F32)], axis=0)
            high, low = split_bf16(square)
            for h in range(3):
                cols = slice(h * 128, h * 128 + 128)
                if j == 2:
                    sv_v[h, 0:128, :] = high[:, cols]
                    sv_v[h, 128:256, :] = low[:, cols]
                else:
                    target = tq_v if j == 0 else tk_v
                    target[cols, 0:128] = mm_nt(perm_b, high[:, cols]).astype(BF16)
                    target[cols, 128:256] = mm_nt(perm_b, low[:, cols]).astype(BF16)

    early = z_at < 3

    @pl.when(early)
    def _():
        prepare()
        project()

    def tell(level):
        for off in (1, -1):
            pl.semaphore_signal(relay.at[level], inc=1, device_id=ahead(off), device_id_type=MESH)

    pl.semaphore_wait(barrier, len(plane) + 3)
    tell(0)
    vel_copy = remote(vel_mine, vel_other, vel_send, vel_recv, (1 - cfg, uly, blk))
    vel_copy.start()
    pl.when(jnp.logical_not(early))(prepare)

    gains = jnp.concatenate([gains_v[...], jnp.zeros((6, 128), F32)], axis=0)
    gains = mm_nt(perm, gains, precision=lax.Precision.HIGHEST)
    ga_q = gains[0:64, 0:1] * (math.log2(math.e) / math.sqrt(HEAD_DIM))
    gb_q = gains[64:128, 0:1] * (math.log2(math.e) / math.sqrt(HEAD_DIM))
    ga_k = gains[0:64, 1:2]
    gb_k = gains[64:128, 1:2]

    step = index_s[0]
    scale_now = guid_s[step]
    step_now = size_s[step]
    vel_copy.wait()
    mine = vel_mine[...]
    other = vel_other[...]
    cond = jnp.where(cfg == 0, mine, other)
    uncond = jnp.where(cfg == 0, other, mine)
    guided = uncond + scale_now * (cond - uncond)
    guided = jnp.concatenate([guided[:, 0:64], guided[:, 64:128]], axis=0)
    latent = latent_v[...] - step_now * guided
    next_ref[...] = latent
    power = jnp.dot(latent, gram_v[...], precision=lax.Precision.HIGHEST, preferred_element_type=F32)
    var = jnp.maximum(jnp.sum(power * latent, axis=1, keepdims=True), 0.0)
    normed = (latent * lax.rsqrt(var + EPS)).astype(BF16)
    own_at = ((core * n_x + x_at) * n_y + y_at) * 32
    own_rows = pl.ds(pl.multiple_of(own_at, 32), 32)
    own_half = pl.ds(pl.multiple_of(core * half_rows, half_rows), half_rows)
    sib_half = pl.ds(pl.multiple_of((1 - core) * half_rows, half_rows), half_rows)
    xp_v[0, own_rows, :] = jnp.concatenate([normed[0:32], normed[32:64]], axis=1)

    def rows_of(dx, dy, dc):
        at = ((core + dc) % 2 * n_x + (x_at + n_x - dx) % n_x) * n_y + (y_at + dy) % n_y
        return pl.ds(pl.multiple_of(at * 32, 32), 32)

    def offset(r):
        return (r + 1) // 2 * (2 * (r % 2) - 1)

    def z_copy(r):
        src = xp_v.at[0, own_rows, :]
        dst = xp_v.at[r, own_rows, :]
        return remote(src, dst, z_send.at[r - 1], z_recv.at[r - 1], ahead(-offset(r)))

    def plane_copy(k):
        there = xp_v.at[0, own_rows, :]
        return remote(there, there, plane_send.at[k], plane_recv.at[k], near(*plane[k]))

    def plane_from(k):
        there = xp_v.at[0, rows_of(*plane[k]), :]
        return remote(there, there, plane_send.at[k], plane_recv.at[k], near(*plane[k]))

    def group_copy(g, k):
        first, last = groups[g]
        there = xp_v.at[first : last + 1, own_rows, :]
        return remote(there, there, group_send.at[g, k], group_recv.at[g, k], near(*side[k]))

    def group_from(g, k):
        first, last = groups[g]
        there = xp_v.at[first : last + 1, rows_of(*side[k]), :]
        return remote(there, there, group_send.at[g, k], group_recv.at[g, k], near(*side[k]))

    def sib_copy(g):
        first, last = groups[g]
        there = xp_v.at[first : last + 1, own_half, :]
        return remote(there, there, sib_send.at[g], sib_recv.at[g], (cfg, sib, blk))

    def sib_from(g):
        first, last = groups[g]
        there = xp_v.at[first : last + 1, sib_half, :]
        return remote(there, there, sib_send.at[g], sib_recv.at[g], (cfg, sib, blk))

    def spread(g):
        first, last = groups[g]
        for r in range(first, last + 1):
            z_copy(r).wait_recv()
        for k in range(len(side)):
            group_copy(g, k).start()

    def share(g):
        for k in range(len(side)):
            group_from(g, k).wait_recv()
        sib_copy(g).start()

    for r in range(1, 3):
        z_copy(r).start()
    pl.semaphore_wait(relay.at[0], 2)
    tell(1)
    for k in range(len(plane)):
        plane_copy(k).start()
    pl.semaphore_wait(relay.at[1], 2)
    tell(2)
    for r in range(3, n_z - 1):
        z_copy(r).start()
    pl.semaphore_wait(relay.at[2], 2)
    z_copy(n_z - 1).start()

    pl.when(jnp.logical_not(early))(project)

    for i in range(9, 13):
        loads[i].wait()
    one_hot = jnp.where(lax.broadcasted_iota(jnp.int32, (1, 128), 1) == 64, 1.0, 0.0)
    low_lanes = lax.broadcasted_iota(jnp.int32, (1, 128), 1) < 64

    def unpack(value):
        wide = value.astype(F32)
        first = jnp.where(low_lanes, wide, one_hot).astype(BF16)
        second = jnp.where(low_lanes, pltpu.roll(wide, 64, 1), one_hot).astype(BF16)
        return first, second

    def rope_tabs(ga, gb, cosine, sine):
        return ga * cosine, gb * sine, ga * sine, gb * cosine

    def rotate(proj, t1, t2, t3, t4):
        a, b = proj[0:64], proj[64:128]
        power = jnp.sum(a * a + b * b, axis=0, keepdims=True) * (1.0 / HEAD_DIM)
        scale = lax.rsqrt(power + EPS)
        return (a * t1 - b * t2) * scale, (a * t3 + b * t4) * scale

    def laid(time, rest, times):
        return jnp.concatenate([time, jnp.concatenate([rest] * times, axis=1)], axis=0)

    def make_keys(r):
        halves = unpack(xp_v[r])
        at = (z_at + n_z + offset(r)) % n_z
        size = 2 * half_rows
        times = rope_tabs(ga_k[0:8], gb_k[0:8], ktime_v[0], ktime_v[1])
        for half in range(2):
            cols = slice(half * size, half * size + size)
            aug_v[r, cols, :] = halves[half]
            proj = mm_nt(tk_v[...], jnp.concatenate([halves[half]] * 2, axis=1))
            rests = rope_tabs(ga_k[8:64], gb_k[8:64], ktab_v[at, half, 0, 8:64], ktab_v[at, half, 1, 8:64])
            tabs = [laid(t, r, size // 128) for t, r in zip(times, rests)]
            for h in range(3):
                ka, kb = rotate(proj[h * 128 : h * 128 + 128], *tabs)
                kt_v[r, h, 0:64, cols] = ka.astype(BF16)
                kt_v[r, h, 64:128, cols] = kb.astype(BF16)

    def attend(h, r, rows=slice(None)):
        scores = mm(q_v[h, rows], kt_v[r, h])
        return mm(jnp.exp2(scores).astype(BF16), aug_v[r])

    spread(0)
    for k in range(len(plane)):
        plane_from(k).wait_recv()

    parts = []
    for dx in leave:
        for c in range(2):
            at = (c * n_x + (x_at + dx) % n_x) * n_y + y_at
            parts += list(unpack(xp_v[0, pl.ds(pl.multiple_of(at * 32, 32), 32), :]))
    rows_q = jnp.concatenate(parts, axis=0)
    proj = mm_nt(tq_v[...], jnp.concatenate([rows_q, rows_q], axis=1))
    here = [pl.ds(pl.multiple_of((x_at + dx) % n_x * 128, 128), 128) for dx in leave]
    cos_t, sin_t = [jnp.concatenate([qtime_v[i, :, lanes] for lanes in here], axis=1) for i in range(2)]
    times = rope_tabs(ga_q[0:8], gb_q[0:8], cos_t, sin_t)
    rests = rope_tabs(ga_q[8:64], gb_q[8:64], qtab_v[0, 8:64], qtab_v[1, 8:64])
    tabs = [laid(t, r, n_uly * 64 // 128) for t, r in zip(times, rests)]
    for h in range(3):
        qa, qb = rotate(proj[h * 128 : h * 128 + 128], *tabs)
        q_v[h] = jnp.transpose(jnp.concatenate([qa, qb], axis=0)).astype(BF16)

    make_keys(0)
    acc_v[0] = attend(0, 0)
    spread(1)
    acc_v[1] = attend(1, 0)
    share(0)
    acc_v[2] = attend(2, 0)
    sib_from(0).wait_recv()

    make_keys(1)
    for h in range(2):
        acc_v[h] += attend(h, 1)
    make_keys(2)
    acc_v[2] += attend(2, 1)
    acc_v[0] += attend(0, 2)
    share(1)
    for h in range(1, 3):
        acc_v[h] += attend(h, 2)
    sib_from(1).wait_recv()
    make_keys(3)
    for h in range(3):
        acc_v[h] += attend(h, 3)
    for r in range(4, n_z):
        make_keys(r)

    width = 3 * HEAD_DIM

    def out_copy(j, dc, h=None):
        c = (core + dc) % 2
        rows = pl.ds(pl.multiple_of(j * 128 + c * 64, 64), 64)
        first, size = (0, width) if h is None else (h * 128, 128)
        src = stage_v.at[rows, first : first + size]
        dst = out_ref.at[:, pl.ds(pl.multiple_of(uly * width + first, 128), size)]
        if leave[j] + dc == 0:
            return pltpu.make_async_copy(src, dst, own_sem)
        to = (x_at + leave[j]) % n_x * 2 + c
        sem = (h or 0, j, dc)
        return remote(src, dst, out_send.at[sem], out_recv.at[sem], (cfg, to, blk))

    def out_from(j, dc, h=None):
        source = (x_at + n_x - leave[j]) % n_x * 2 + (core + dc) % 2
        first, size = (0, width) if h is None else (h * 128, 128)
        src = stage_v.at[0:64, first : first + size]
        dst = out_ref.at[:, pl.ds(pl.multiple_of(source * width + first, 128), size)]
        sem = (h or 0, j, dc)
        return remote(src, dst, out_send.at[sem], out_recv.at[sem], (cfg, source, blk))

    sends = [(0, 0, None), (0, 1, None), (1, 0, None), (1, 1, None)]
    sends += [(2, dc, h) for h in range(3) for dc in range(2)] + [(3, 1, None)]
    def finish(rows, h):
        numer = acc_v[h, rows]
        for r in range(4, n_z):
            numer += attend(h, r, rows)
        mean_x = numer * (1.0 / numer[:, 64:65])
        high, low = split_bf16(mean_x)
        result = mm(jnp.concatenate([high, high], axis=1), sv_v[h]) + mm(low, sv_v[h, 0:128])
        stage_v[rows, h * 128 : h * 128 + 128] = result.astype(BF16)

    for h in range(3):
        finish(slice(0, 256), h)
    for j in range(2):
        for dc in (1, 0):
            out_copy(j, dc).start()
    for h in range(2):
        finish(slice(256, 512), h)
        for dc in (1, 0):
            out_copy(2, dc, h).start()
    finish(slice(256, 384), 2)
    for dc in (1, 0):
        out_copy(2, dc, 2).start()
    finish(slice(384, 512), 2)
    for dc in (1, 0):
        out_copy(3, dc).start()

    for k in range(len(plane)):
        plane_copy(k).wait_send()
    for r in range(1, n_z):
        z_copy(r).wait_send()
    for g in range(len(groups)):
        for k in range(len(side)):
            group_copy(g, k).wait_send()
        sib_copy(g).wait_send()
    out_copy(3, 0).wait()
    for j, dc, h in sends:
        out_copy(j, dc, h).wait_send()
        out_from(j, dc, h).wait_recv()


def hand_over(next_in, out_in, next_ref, out_ref, sems):
    copies = [
        pltpu.make_async_copy(out_in, out_ref, sems.at[0]),
        pltpu.make_async_copy(next_in, next_ref, sems.at[1]),
    ]
    for copy in copies:
        copy.start()
    for copy in copies:
        copy.wait()


def solution(mesh):
    n_uly = mesh.shape["uly"]
    n_blk = mesh.shape["blk"]
    n_y = 2
    n_z = n_blk // n_y
    tables = rope_tables(n_uly, n_y, n_z)

    def on_device(
        hidden, final_mod, final_weight, latent, guidance, step_size, step_index, embed_weight, block_mod, qkv_weight, qk_gains
    ):
        smem = pl.BlockSpec(memory_space=pltpu.SMEM)
        vmem = pl.BlockSpec(memory_space=pltpu.VMEM)
        anywhere = pl.BlockSpec(memory_space=pl.ANY)
        rows, width = hidden.shape[1:]
        cols = qkv_weight.shape[2]
        heads = cols // HEAD_DIM
        keys = 64 * n_uly * n_y
        queries = rows * n_uly
        dma = pltpu.SemaphoreType.DMA
        next_latent, attention = pl.pallas_call(
            functools.partial(kernel, n_uly, n_y, n_z),
            out_shape=(pltpu.VMEM((rows, CHAN), F32), pltpu.VMEM((rows, width), BF16)),
            in_specs=[smem] * 3 + [anywhere] * 7 + [vmem] + [anywhere] * 4,
            out_specs=(vmem, vmem),
            scratch_shapes=[
                pltpu.VMEM((rows, width), BF16),
                pltpu.VMEM((2, width), F32),
                pltpu.VMEM((CHAN, width), BF16),
                pltpu.VMEM((rows, CHAN), F32),
                pltpu.VMEM((CHAN, width), F32),
                pltpu.VMEM((2, width), F32),
                pltpu.VMEM((3, width, cols), BF16),
                pltpu.VMEM(tables[0].shape, F32),
                pltpu.VMEM(tables[1].shape, F32),
                pltpu.VMEM(tables[2].shape[1:], F32),
                pltpu.VMEM(tables[3].shape, F32),
                pltpu.VMEM((32, 128), F32),
                pltpu.VMEM((32, 128), F32),
                pltpu.VMEM((n_z, n_uly * n_y * 32, 128), BF16),
                pltpu.VMEM((144, width), BF16),
                pltpu.VMEM((CHAN, CHAN), F32),
                pltpu.VMEM((cols, 256), BF16),
                pltpu.VMEM((cols, 256), BF16),
                pltpu.VMEM((heads, 256, 128), BF16),
                pltpu.VMEM((n_z, keys, 128), BF16),
                pltpu.VMEM((n_z, heads, 128, keys), BF16),
                pltpu.VMEM((heads, queries, 128), BF16),
                pltpu.VMEM((heads, queries, 128), F32),
                pltpu.VMEM((queries, cols), BF16),
                dma((13,)),
                dma,
                dma,
                dma((n_uly * n_y - 1,)),
                dma((n_uly * n_y - 1,)),
                dma((n_z - 1,)),
                dma((n_z - 1,)),
                dma((2, n_uly // 2 * n_y - 1)),
                dma((2, n_uly // 2 * n_y - 1)),
                dma((2,)),
                dma((2,)),
                dma((heads, n_uly // 2, 2)),
                dma((heads, n_uly // 2, 2)),
                dma,
                pltpu.SemaphoreType.REGULAR((n_z // 2 - 1,)),
            ],
            compiler_params=pltpu.CompilerParams(
                collective_id=0, has_side_effects=True, vmem_limit_bytes=56 << 20
            ),
        )(
            guidance,
            step_size,
            step_index,
            hidden[0],
            final_mod[0],
            final_weight.T,
            latent,
            embed_weight,
            block_mod[0],
            jnp.transpose(qkv_weight, (1, 0, 2)),
            qk_gains,
            *[jnp.asarray(t) for t in tables],
        )
        next_latent, attention = pl.pallas_call(
            hand_over,
            out_shape=(
                jax.ShapeDtypeStruct((rows, CHAN), F32),
                jax.ShapeDtypeStruct((rows, width), BF16),
            ),
            in_specs=[vmem] * 2,
            out_specs=(anywhere, anywhere),
            scratch_shapes=[dma((2,))],
        )(
            pltpu.with_memory_space_constraint(next_latent, pltpu.VMEM),
            pltpu.with_memory_space_constraint(attention, pltpu.VMEM),
        )
        return (next_latent, attention[None])

    return jax.shard_map(
        on_device,
        mesh=mesh,
        in_specs=(
            P("cfg", ("uly", "blk"), None),
            P("cfg", None, None),
            P(),
            P(("uly", "blk"), None),
            P(),
            P(),
            P(),
            P(),
            P("cfg", None, None),
            P(None, None, "uly"),
            P(),
        ),
        out_specs=(P(("uly", "blk"), None), P("cfg", ("uly", "blk"), None)),
        check_vma=False,
    )
```
